32 devices in a mesh: img: 2 (over x), py: 4 (over y, core), px: 4 (over z).
Axes of the slice: x: 2, y: 2, z: 4, core: 2. Of those that a mesh axis runs over, the one named last changes fastest.
Arguments:
- queries: bfloat16 [2, 64, 64, 1536], P('img', 'py', 'px')
- keys: bfloat16 [2, 64, 64, 1536], P('img', 'py', 'px')
- values: bfloat16 [2, 64, 64, 1536], P('img', 'py', 'px'), may hold values from -6 to 6
- pattern: int32 [2, 8, 8, 9], P('img', 'py', 'px'), may hold values from 0 to 1, as said below
- targets: int32 [2, 8, 8, 12, 3], P('img', 'py', 'px'), may hold values from 0 to 8, as said below
- router_q: float32 [12, 128, 64], replicated, may hold values from -1.5 to 1.5
- router_k: float32 [12, 128, 64], replicated, may hold values from -1.5 to 1.5
Outputs:
- attended: bfloat16 [2, 64, 64, 1536], P('img', 'py', 'px')
- grad_q: float32 [12, 128, 64], replicated
- grad_k: float32 [12, 128, 64], replicated
The draws below stay inside these ranges and needn't reach their ends.
Inputs may be any that keep to these rules, and one draw needn't show every extreme that they name: `pattern`: the centre offset and the offsets one block away along one axis that lie in the image are 1; offsets outside the image are 0. `targets`: 3 different offsets per query block and head, each with pattern 1.
All inputs are finite; a program needn't handle non-finite values.
Results may differ from the reference program's by a relative error of at most 0.0049.
Values may be sent and summed in bfloat16 or wider, within the bound.
A program may use at most 64 MiB of HBM per device.

```python
import math
import jax
import jax.numpy as jnp
from jax import lax

HEADS = 12
DH = 128
RW = 64
BS = 8
RADIUS = 1
TOPK = 3
NOFF = 9
FEAT = 1536
IMAGES = 2
NBY = 8
NBX = 8
NY = 64
NX = 64


def draw_field(key, salt):
    base_key = jax.random.fold_in(key, salt)
    shape = (IMAGES, NY, NX, FEAT)
    base = jax.random.normal(base_key, shape, jnp.float32)
    base = jnp.clip(base, -6.0, 6.0)
    return base.astype(jnp.bfloat16)


def draw_queries(key, part):
    return draw_field(key, 11)


def draw_keys(key, part):
    return draw_field(key, 12)


def block_layout(key):
    width = 2 * RADIUS + 1
    rows = jnp.arange(NBY, dtype=jnp.int32)[:, None, None]
    cols = jnp.arange(NBX, dtype=jnp.int32)[None, :, None]
    offs = jnp.arange(NOFF, dtype=jnp.int32)
    shift_y = offs // width - RADIUS
    shift_x = offs % width - RADIUS
    inside = (rows + shift_y >= 0) & (rows + shift_y < NBY) & (cols + shift_x >= 0) & (cols + shift_x < NBX)
    core = jnp.abs(shift_y) + jnp.abs(shift_x) <= 1
    coin = jax.random.randint(jax.random.fold_in(key, 201), (IMAGES, NBY, NBX, NOFF), 0, 8)
    live = inside[None] & (core[None, None, None, :] | (coin < 5))
    return live.astype(jnp.int32)


def draw_pattern(key, part):
    return block_layout(key)


def draw_targets(key, part):
    live = block_layout(key)
    noise = jax.random.randint(jax.random.fold_in(key, 202), (IMAGES, NBY, NBX, HEADS, NOFF), 0, 2 ** 20)
    offs = jnp.arange(NOFF, dtype=jnp.int32)
    score = noise * 32 + offs + live[:, :, :, None, :] * 2 ** 26
    return lax_top(score)


def lax_top(score):
    return jax.lax.top_k(score, TOPK)[1].astype(jnp.int32)


def levels(key, shape, cuts, least, top_value):
    def one(axis_at, parts):
        heights = jax.random.uniform(jax.random.fold_in(jax.random.fold_in(key, 6), axis_at), (parts,), jnp.float32, least / len(cuts), top_value / len(cuts))
        return jnp.repeat(jnp.exp(heights), shape[axis_at] // parts).reshape((-1,) + (1,) * (len(shape) - axis_at - 1))

    loudness = one(*cuts[0])
    for cut in cuts[1:]:
        loudness = loudness * one(*cut)
    return loudness


def scatter_about(own_key, extent, spread, bound, shards=(), held_as=jnp.bfloat16):
    values = jax.random.normal(own_key, extent, jnp.float32) * spread
    if len(shards) > 0:
        values = levels(own_key, extent, shards, -0.22, 0.18) * values
    return jnp.clip(values, min=-bound, max=bound).astype(held_as)


def setup_inputs(seed: int = 0) -> dict:
    key_of = jax.random.split(jax.random.key(seed), 8)
    queries = draw_queries(jax.random.fold_in(key_of[7], 71), 0)
    keys = draw_keys(jax.random.fold_in(key_of[7], 71), 0)
    values = scatter_about(key_of[2], (IMAGES, NY, NX, FEAT), 1.0, 6.0, ((0, 2), (1, 4), (2, 4)))
    pattern = draw_pattern(jax.random.fold_in(key_of[7], 71), 0)
    targets = draw_targets(jax.random.fold_in(key_of[7], 71), 0)
    router_q = scatter_about(key_of[5], (HEADS, DH, RW), (DH // 8) ** -0.5, 1.5, (), jnp.float32)
    router_k = scatter_about(key_of[6], (HEADS, DH, RW), (DH // 8) ** -0.5, 1.5, (), jnp.float32)
    return dict(queries=queries, keys=keys, values=values, pattern=pattern, targets=targets, router_q=router_q, router_k=router_k)


def attend(query_tile, key_ext, value_ext, live):
    tile_y, tile_x, feat = query_tile.shape
    blocks_y = tile_y // BS
    blocks_x = tile_x // BS
    width = 2 * RADIUS + 1
    side = width * BS
    scale = 1.0 / math.sqrt(DH)
    anchor = jnp.zeros((), jnp.int32)

    def regroup(window):
        return window.reshape(width, BS, width, BS, feat).transpose(0, 2, 1, 3, 4).reshape(NOFF * BS * BS, HEADS, DH)

    def one_block(index):
        row = (index // blocks_x).astype(jnp.int32)
        col = (index % blocks_x).astype(jnp.int32)
        start_y = (row * BS).astype(jnp.int32)
        start_x = (col * BS).astype(jnp.int32)
        query = lax.dynamic_slice(query_tile, (start_y, start_x, anchor), (BS, BS, feat)).reshape(BS * BS, HEADS, DH)
        window_k = regroup(lax.dynamic_slice(key_ext, (start_y, start_x, anchor), (side, side, feat)))
        window_v = regroup(lax.dynamic_slice(value_ext, (start_y, start_x, anchor), (side, side, feat)))
        mask_row = lax.dynamic_slice(live, (row, col, anchor), (1, 1, NOFF)).reshape(NOFF)
        key_mask = jnp.repeat(mask_row, BS * BS) > 0
        scores = jnp.einsum('qhd,khd->hqk', query, window_k, preferred_element_type=jnp.float32) * scale
        scores = jnp.where(key_mask[None, None, :], scores, -1e+30)
        top = lax.optimization_barrier(jnp.max(scores, axis=-1, keepdims=True))
        weights = jnp.exp(scores - top)
        probs = (weights / lax.optimization_barrier(jnp.sum(weights, axis=-1, keepdims=True))).astype(jnp.bfloat16)
        out = jnp.einsum('hqk,khd->qhd', probs, window_v, preferred_element_type=jnp.float32)
        return out.astype(jnp.bfloat16).reshape(BS, BS, feat)
    outs = lax.map(one_block, jnp.arange(blocks_y * blocks_x, dtype=jnp.int32))
    return outs.reshape(blocks_y, blocks_x, BS, BS, feat).transpose(0, 2, 1, 3, 4).reshape(tile_y, tile_x, feat)

def pooling(tile):
    tile_y, tile_x, feat = tile.shape
    shaped = tile.reshape(tile_y // BS, BS, tile_x // BS, BS, HEADS, DH)
    return lax.optimization_barrier(jnp.sum(shaped, axis=(1, 3), dtype=jnp.float32)) / (BS * BS)

def router_loss(weights_q, weights_k, pooled_q, pooled_k, live, chosen):
    route_q = jnp.einsum('yxhd,hdr->yxhr', pooled_q, weights_q, precision=lax.Precision.HIGHEST)
    route_k = jnp.einsum('yxhd,hdr->yxhr', pooled_k, weights_k, precision=lax.Precision.HIGHEST)
    blocks_y, blocks_x = (pooled_q.shape[0], pooled_q.shape[1])
    width = 2 * RADIUS + 1
    shifted = jnp.stack([route_k[up:up + blocks_y, left:left + blocks_x] for up in range(width) for left in range(width)], axis=2)
    logits = jnp.einsum('yxhr,yxohr->yxho', route_q, shifted, precision=lax.Precision.HIGHEST) / math.sqrt(RW)
    logits = jnp.where(live[:, :, None, :] > 0, logits, -1e+30)
    top = lax.optimization_barrier(jnp.max(logits, axis=-1, keepdims=True))
    logz = top + jnp.log(lax.optimization_barrier(jnp.sum(jnp.exp(logits - top), axis=-1, keepdims=True)))
    logp = logits - logz
    picks = (chosen[..., None] == jnp.arange(NOFF, dtype=jnp.int32)).astype(jnp.float32)
    return -jnp.sum(picks * logp[:, :, :, None, :])

def reference(queries, keys, values, pattern, targets, router_q, router_k):
    rim = RADIUS * BS

    def image_out(items):
        query_img, key_img, value_img, live = items
        key_pad = jnp.pad(key_img, ((rim, rim), (rim, rim), (0, 0)))
        value_pad = jnp.pad(value_img, ((rim, rim), (rim, rim), (0, 0)))
        return attend(query_img, key_pad, value_pad, live)
    attended = lax.map(image_out, (queries, keys, values, pattern))
    pooled_q = lax.map(pooling, queries)
    pooled_k = lax.map(pooling, keys)
    pooled_k = jnp.pad(pooled_k, ((0, 0), (RADIUS, RADIUS), (RADIUS, RADIUS), (0, 0), (0, 0)))
    normal = float(TOPK * HEADS * NBY * NBX)

    def total_loss(weights_q, weights_k):

        def one_image(items):
            pq, pk, live, chosen = items
            return router_loss(weights_q, weights_k, pq, pk, live, chosen)
        return jnp.sum(lax.map(one_image, (pooled_q, pooled_k, pattern, targets))) / normal
    grad_q, grad_k = jax.grad(total_loss, argnums=(0, 1))(router_q, router_k)
    return (attended, grad_q, grad_k)
```

```python
import functools
import math

import jax
import jax.numpy as jnp
from jax import lax
from jax.experimental import pallas as pl
from jax.experimental.pallas import tpu as pltpu
from jax.sharding import PartitionSpec as P

HEADS = 12
DH = 128
RW = 64
BS = 8
TOPK = 3
NOFF = 9
HG = 2
NG = HEADS // HG
GL = HG * DH
WINDOW = 3
BB = BS * BS
DEAD = -1e30
LIVE = 3e38
MESH = pl.DeviceIdType.MESH
F32 = jnp.float32
BF16 = jnp.bfloat16
HIGH = lax.Precision.HIGHEST


def lanes(start, size):
    return pl.ds(pl.multiple_of(start, DH), size)


def tile_blocks(x):
    return [x[by * BS:(by + 1) * BS, bx * BS:(bx + 1) * BS] for by in range(2) for bx in range(2)]


def dot_t(a, b):
    return lax.dot_general(a, b, (((1,), (1,)), ((), ())), preferred_element_type=F32)


def kernel(
    sizes, q_ref, k_ref, v_ref, pat_ref, tgt_ref, wq_ref, wk_ref,
    out_ref, gq_ref, gk_ref,
    q_s, zs, zr, yr, cr, acc, den, top, cap_a, cap_b, msg, pool, xbuf, gbuf,
    zs_sem, zr_sem, ys_sem, yr_sem, cs_sem, cr_sem,
    ms_sem, mr_sem, xs_sem, xr_sem, gs_sem, gr_sem, hs_sem, hr_sem,
):
    ni, npy, npx = sizes
    per_py = HEADS // npy
    group = npy * npx
    img = lax.axis_index("img")
    py = lax.axis_index("py")
    px = lax.axis_index("px")
    me = py * npx + px
    has_x = (px > 0, px < npx - 1)
    has_y = (py > 0, py < npy - 1)
    to_x = (px - 1, px + 1)
    to_y = (py - 1, py + 1)

    barrier = pltpu.get_barrier_semaphore()
    for d in range(1, group):
        other = lax.rem(me + d, group)
        pl.semaphore_signal(
            barrier, inc=1,
            device_id={"py": lax.div(other, npx), "px": lax.rem(other, npx)},
            device_id_type=MESH,
        )
    for d in range(1, ni):
        pl.semaphore_signal(
            barrier, inc=1, device_id={"img": lax.rem(img + d, ni)}, device_id_type=MESH
        )

    def z_copy(side, g):
        return pltpu.make_async_remote_copy(
            src_ref=zs.at[side, g], dst_ref=zr.at[1 - side, g],
            send_sem=zs_sem.at[side, g], recv_sem=zr_sem.at[1 - side, g],
            device_id={"px": to_x[side]}, device_id_type=MESH,
        )

    def z_arrival(side, g):
        return pltpu.make_async_remote_copy(
            src_ref=zs.at[side, g], dst_ref=zr.at[side, g],
            send_sem=zs_sem.at[side, g], recv_sem=zr_sem.at[side, g],
            device_id={"px": to_x[side]}, device_id_type=MESH,
        )

    def y_rows(which, side, g):
        ref = (k_ref, v_ref)[which]
        return ref.at[pl.ds(side * BS, BS), :, lanes(g * GL, GL)]

    def y_copy(which, side, g, slot):
        return pltpu.make_async_remote_copy(
            src_ref=y_rows(which, side, g), dst_ref=yr.at[slot, g, which],
            send_sem=ys_sem.at[side, which, g], recv_sem=yr_sem.at[slot, which, g],
            device_id={"py": to_y[side]}, device_id_type=MESH,
        )

    def c_copy(side_y, side_x, g, slot):
        return pltpu.make_async_remote_copy(
            src_ref=zr.at[side_x, g, :, pl.ds(side_y * BB, BB)],
            dst_ref=cr.at[slot, side_x, g],
            send_sem=cs_sem.at[side_y, side_x, g], recv_sem=cr_sem.at[slot, side_x, g],
            device_id={"py": to_y[side_y]}, device_id_type=MESH,
        )

    def send_z(g):
        for side in range(2):
            @pl.when(has_x[side])
            def _():
                z_copy(side, g).start()

    def send_y(g):
        for side in range(2):
            @pl.when(has_y[side])
            def _():
                for which in range(2):
                    y_copy(which, side, g, 1 - side).start()

    def cap_of(block, dy, dx):
        by, bx = divmod(block, 2)
        off = (dy + 1) * 3 + dx + 1
        return jnp.where(pat_ref[0, by, bx, off] > 0, F32(LIVE), F32(DEAD))

    lane_a = lax.broadcasted_iota(jnp.int32, (BS, 4 * BB), 1)
    lane_b = lax.broadcasted_iota(jnp.int32, (BS, 2 * BB), 1)
    for block in range(4):
        by, bx = divmod(block, 2)
        sy, sx = 2 * by - 1, 2 * bx - 1
        col_a = lax.rem(lax.div(lane_a, BS), 2)
        col_b = lax.rem(lax.div(lane_b, BS), 2)

        def pick(row, col, a, b):
            return jnp.where(col > 0, b, a)

        rows = [
            jnp.where(col_a > 0, cap_of(block, r - by, 1 - bx), cap_of(block, r - by, -bx))
            for r in range(2)
        ]
        cap_a[block] = jnp.where(lane_a >= 2 * BB, rows[1], rows[0])
        cap_b[block, :, 0:128] = jnp.where(
            lane_b >= BB, cap_of(block, 1 - by, sx), cap_of(block, -by, sx)
        )
        cap_b[block, :, 128:256] = jnp.where(
            col_b > 0, cap_of(block, sy, 1 - bx), cap_of(block, sy, -bx)
        )
        corner = cap_of(block, sy, sx)
        if bx == 0:
            cap_b[block, :, 256:384] = jnp.where(lane_b >= BB, F32(DEAD), corner)
        else:
            cap_b[block, :, 256:384] = jnp.where(lane_b >= BB, corner, F32(DEAD))

    def prepare(g, carry):
        for j in range(HG):
            h = g * HG + j
            hl = lanes(h * DH, DH)
            jl = pl.ds(j * DH, DH)
            q = q_ref[:, :, hl].astype(F32)
            k = k_ref[:, :, hl].astype(F32)
            v = v_ref[:, :, hl].astype(F32)
            parts = tile_blocks(q)
            q_s[h] = jnp.concatenate([b.reshape(BB, DH) for b in parts], axis=0).astype(BF16)
            for b in range(4):
                msg[h, b:b + 1, :] = jnp.sum(
                    jnp.sum(parts[b], axis=0), axis=0, keepdims=True) / BB
            parts = tile_blocks(k)
            for b in range(4):
                msg[h, 4 + b:5 + b, :] = jnp.sum(
                    jnp.sum(parts[b], axis=0), axis=0, keepdims=True) / BB
            for side in range(2):
                sl = slice(side * BS, (side + 1) * BS)
                zs[side, g, 0, :, jl] = k[:, sl, :].reshape(2 * BB, DH).astype(BF16)
                zs[side, g, 1, :, jl] = v[:, sl, :].reshape(2 * BB, DH).astype(BF16)
        return carry

    lax.fori_loop(0, NG, prepare, 0)

    lane = lax.broadcasted_iota(jnp.int32, (1, DH), 1)
    code_rows = []
    for block in range(4):
        by, bx = divmod(block, 2)
        row = jnp.full((1, DH), -1.0, F32)
        for o in range(NOFF):
            row = jnp.where(
                lane == o, jnp.where(pat_ref[0, by, bx, o] > 0, F32(0.0), F32(-1.0)), row)
        code_rows.append(row)

    def encode(h, carry):
        for block in range(4):
            by, bx = divmod(block, 2)
            chosen = lane == tgt_ref[0, by, bx, h, 0]
            for t in range(1, TOPK):
                chosen = chosen | (lane == tgt_ref[0, by, bx, h, t])
            row = jnp.where(code_rows[block] < 0, F32(-1.0), jnp.where(chosen, F32(1.0), F32(0.0)))
            msg[h, 8 + block:9 + block, :] = row
        msg[h, 12:16, :] = jnp.zeros((4, DH), F32)
        return carry

    lax.fori_loop(0, HEADS, encode, 0)

    for side in range(2):
        @pl.when(jnp.logical_not(has_x[side]))
        def _():
            zr[side] = jnp.zeros(zr.shape[1:], BF16)
        @pl.when(jnp.logical_not(has_y[side]))
        def _():
            yr[side] = jnp.zeros(yr.shape[1:], BF16)
        for other in range(2):
            @pl.when(jnp.logical_not(has_y[side] & has_x[other]))
            def _():
                cr[side, other] = jnp.zeros(cr.shape[2:], BF16)

    pl.semaphore_wait(barrier, group - 1 + ni - 1)
    send_z(0)

    def owner_of(h):
        return h // per_py, h % npx

    def m_copy(h, slot):
        oy, ox = owner_of(h)
        return pltpu.make_async_remote_copy(
            src_ref=msg.at[h], dst_ref=pool.at[slot],
            send_sem=ms_sem.at[h], recv_sem=mr_sem.at[slot],
            device_id={"py": oy, "px": ox}, device_id_type=MESH,
        )

    for h in range(HEADS):
        oy, ox = owner_of(h)
        @pl.when(jnp.logical_not((py == oy) & (px == ox)))
        def _():
            m_copy(h, me).start()
    turn = lax.rem(px + npx * HEADS - py * per_py, npx)
    own = turn < per_py
    my_head = jnp.minimum(py * per_py + turn, HEADS - 1)

    send_y(0)
    for g in range(1, WINDOW):
        send_z(g)
        send_y(g)

    scale = math.log2(math.e) / math.sqrt(DH)
    ones = jnp.ones((2 * DH, DH), BF16)

    def local_heads(g, carry):
        for j in range(HG):
            h = g * HG + j
            hl = lanes(h * DH, DH)
            key = k_ref[:, :, hl].reshape(4 * BB, DH)
            val = v_ref[:, :, hl].reshape(4 * BB, DH)
            s = dot_t(q_s[h], key)
            s = jnp.minimum(s.reshape(4, BS, BS, 4 * BB), cap_a[...][:, None]).reshape(4 * BB, 4 * BB)
            m = jnp.max(s, axis=-1, keepdims=True)
            p = jnp.exp2((s - m) * scale).astype(BF16)
            r = jnp.dot(p, jnp.concatenate([val, ones], axis=1), preferred_element_type=F32)
            acc[h] = r[:, :DH]
            den[h] = r[:, DH:]
            top[h] = jnp.broadcast_to(m, (4 * BB, DH))
        return carry

    lax.fori_loop(0, NG // 2, local_heads, 0)

    def x_copy(d):
        return pltpu.make_async_remote_copy(
            src_ref=xbuf.at[img], dst_ref=xbuf.at[img],
            send_sem=xs_sem.at[d], recv_sem=xr_sem.at[d],
            device_id={"img": lax.rem(img + d, ni)}, device_id_type=MESH,
        )

    def x_arrival(d):
        src = lax.rem(img + ni - d, ni)
        return pltpu.make_async_remote_copy(
            src_ref=xbuf.at[src], dst_ref=xbuf.at[src],
            send_sem=xs_sem.at[d], recv_sem=xr_sem.at[d],
            device_id={"img": lax.rem(img + d, ni)}, device_id_type=MESH,
        )

    @pl.when(own)
    def _():
        pool[me] = msg[my_head]
        for src in range(group):
            @pl.when(me != src)
            def _():
                m_copy(0, src).wait_recv()
        nb = 4 * group
        pq = pool[:, 0:4, :].reshape(nb, DH) if False else jnp.concatenate(
            [pool[s, 0:4, :] for s in range(group)], axis=0)
        pk = jnp.concatenate([pool[s, 4:8, :] for s in range(group)], axis=0)
        code = jnp.concatenate([pool[s, 8:12, :] for s in range(group)], axis=0)
        wq = wq_ref[my_head]
        wk = wk_ref[my_head]
        rq = jnp.dot(pq, wq, precision=HIGH, preferred_element_type=F32)
        rk = jnp.dot(pk, wk, precision=HIGH, preferred_element_type=F32)
        logits = lax.dot_general(
            rq, rk, (((1,), (1,)), ((), ())), precision=HIGH, preferred_element_type=F32
        ) / math.sqrt(RW)

        def place(i):
            s = lax.div(i, 4)
            b = lax.rem(i, 4)
            return (
                lax.div(s, npx) * 2 + lax.div(b, 2),
                lax.rem(s, npx) * 2 + lax.rem(b, 2),
            )

        iy, ix = place(lax.broadcasted_iota(jnp.int32, (nb, nb), 0))
        jy, jx = place(lax.broadcasted_iota(jnp.int32, (nb, nb), 1))
        picks = jnp.full((nb, nb), -1.0, F32)
        for o in range(NOFF):
            dy, dx = o // 3 - 1, o % 3 - 1
            picks = jnp.where((jy - iy == dy) & (jx - ix == dx), code[:, o:o + 1], picks)
        live = picks >= 0
        logits = jnp.where(live, logits, DEAD)
        e = jnp.where(live, jnp.exp(logits - jnp.max(logits, axis=-1, keepdims=True)), 0.0)
        prob = e / jnp.sum(e, axis=-1, keepdims=True)
        picks = jnp.where(live, picks, 0.0)
        count = jnp.sum(picks, axis=-1, keepdims=True)
        normal = float(TOPK * HEADS * nb) * math.sqrt(RW)
        dl = jnp.where(live, count * prob - picks, 0.0) / normal
        drq = jnp.dot(dl, rk, precision=HIGH, preferred_element_type=F32)
        drk = lax.dot_general(
            dl, rq, (((0,), (0,)), ((), ())), precision=HIGH, preferred_element_type=F32)
        grads = [
            lax.dot_general(
                a, b, (((0,), (0,)), ((), ())), precision=HIGH, preferred_element_type=F32)
            for a, b in ((pq, drq), (pk, drk))
        ]
        xbuf[img] = jnp.concatenate(grads, axis=1)
        for d in range(1, ni):
            x_copy(d).start()

    lax.fori_loop(NG // 2, NG, local_heads, 0)

    def g_copy(d, head):
        return pltpu.make_async_remote_copy(
            src_ref=gbuf.at[head], dst_ref=gbuf.at[head],
            send_sem=gs_sem.at[d], recv_sem=gr_sem.at[head],
            device_id={"px": lax.rem(px + d, npx)}, device_id_type=MESH,
        )

    def sum_images():
        @pl.when(own)
        def _():
            for d in range(1, ni):
                x_arrival(d).wait_recv()
            total = xbuf[0]
            for i in range(1, ni):
                total = total + xbuf[i]
            gbuf[my_head] = total.astype(BF16)
            for d in range(1, npx):
                g_copy(d, my_head).start()

    def h_copy(bit, start, count, slot):
        mate = py + bit - 2 * bit * lax.rem(lax.div(py, bit), 2)
        return pltpu.make_async_remote_copy(
            src_ref=gbuf.at[pl.ds(start, count)], dst_ref=gbuf.at[pl.ds(start, count)],
            send_sem=hs_sem.at[slot], recv_sem=hr_sem.at[slot],
            device_id={"py": mate}, device_id_type=MESH,
        )

    bits = []
    b = npy // 2
    while b:
        bits.append(b)
        b //= 2

    def held(step):
        found = [py]
        for s in range(step):
            bit = bits[s]
            found = found + [r + bit - 2 * bit * lax.rem(lax.div(r, bit), 2) for r in found]
        return found

    def slots(step):
        return [2 ** step - 1 + i for i in range(2 ** step)]

    def cube_send(step):
        for r, slot in zip(held(step), slots(step)):
            h_copy(bits[step], r * per_py, per_py, slot).start()

    def cube_wait(step):
        bit = bits[step]
        for r, slot in zip(held(step), slots(step)):
            other = r + bit - 2 * bit * lax.rem(lax.div(r, bit), 2)
            h_copy(bit, other * per_py, per_py, slot).wait_recv()

    def gather_px():
        for i in range(per_py):
            head = py * per_py + i
            @pl.when(jnp.logical_not(own & (my_head == head)))
            def _():
                g_copy(1, head).wait_recv()

    def finish_grads():
        for h in range(HEADS):
            g = gbuf[h].astype(F32)
            gq_ref[h] = g[:, :RW]
            gk_ref[h] = g[:, RW:]

    def rim_heads(g):
        for j in range(HG):
            h = g * HG + j
            jl = pl.ds(j * DH, DH)
            q = q_s[h]
            qb = [q[i * BB:(i + 1) * BB] for i in range(4)]
            sx, sy, vx, vy = [], [], [], []
            for side in range(2):
                key = zr[side, g, 0, :, jl]
                sx.append(dot_t(jnp.concatenate([qb[side], qb[2 + side]], axis=0), key))
                vx.append(jnp.concatenate([zr[side, g, 1, :, jl], ones[:2 * BB]], axis=1))
                key = jnp.concatenate(
                    [yr[side, g, 0, :, :, jl].reshape(2 * BB, DH),
                     cr[side, 0, g, 0, :, jl], cr[side, 1, g, 0, :, jl]], axis=0)
                val = jnp.concatenate(
                    [yr[side, g, 1, :, :, jl].reshape(2 * BB, DH),
                     cr[side, 0, g, 1, :, jl], cr[side, 1, g, 1, :, jl]], axis=0)
                sy.append(dot_t(q[side * 2 * BB:(side + 1) * 2 * BB], key))
                vy.append(jnp.concatenate([val, ones], axis=1))
            wx, wy, ms = [], [], []
            for i in range(4):
                by, bx = divmod(i, 2)
                a = sx[bx][by * BB:(by + 1) * BB].reshape(BS, BS, 2 * BB)
                c = sy[by][bx * BB:(bx + 1) * BB].reshape(BS, BS, 4 * BB)
                a = jnp.minimum(a, cap_b[i, :, 0:2 * BB][None]).reshape(BB, 2 * BB)
                c = jnp.minimum(c, cap_b[i, :, 2 * BB:6 * BB][None]).reshape(BB, 4 * BB)
                widest = jnp.maximum(a, jnp.maximum(c[:, :2 * BB], c[:, 2 * BB:]))
                m = jnp.maximum(
                    top[h, i * BB:(i + 1) * BB, :], jnp.max(widest, axis=-1, keepdims=True))
                wx.append(jnp.exp2((a - m) * scale).astype(BF16))
                wy.append(jnp.exp2((c - jnp.concatenate([m, m], axis=1)) * scale).astype(BF16))
                ms.append(m)
            rx = [
                jnp.dot(jnp.concatenate([wx[s], wx[2 + s]], axis=0), vx[s],
                        preferred_element_type=F32)
                for s in range(2)
            ]
            ry = [
                jnp.dot(jnp.concatenate([wy[2 * s], wy[2 * s + 1]], axis=0), vy[s],
                        preferred_element_type=F32)
                for s in range(2)
            ]
            outs = []
            for i in range(4):
                by, bx = divmod(i, 2)
                rows = slice(i * BB, (i + 1) * BB)
                old = jnp.exp2((top[h, rows, :] - ms[i]) * scale)
                r = rx[bx][by * BB:(by + 1) * BB] + ry[by][bx * BB:(bx + 1) * BB]
                num = acc[h, rows, :] * old + r[:, :DH]
                tot = den[h, rows, :] * old + r[:, DH:]
                outs.append((num / tot).reshape(BS, BS, DH))
            for by in range(2):
                out_ref[by * BS:(by + 1) * BS, :, lanes(h * DH, DH)] = jnp.concatenate(
                    [outs[2 * by], outs[2 * by + 1]], axis=1).astype(BF16)

    def advance(s, carry):
        @pl.when(s < NG)
        def _():
            for side in range(2):
                @pl.when(has_x[side])
                def _():
                    z_arrival(side, s).wait_recv()
                for side_y in range(2):
                    @pl.when(has_x[side] & has_y[side_y])
                    def _():
                        c_copy(side_y, side, s, 1 - side_y).start()

            @pl.when(s + WINDOW < NG)
            def _():
                send_z(s + WINDOW)
                send_y(s + WINDOW)

        @pl.when(s >= 1)
        def _():
            g = s - 1
            for side in range(2):
                @pl.when(has_y[side])
                def _():
                    for which in range(2):
                        y_copy(which, side, g, side).wait_recv()
                for side_x in range(2):
                    @pl.when(has_y[side] & has_x[side_x])
                    def _():
                        c_copy(side, side_x, g, side).wait_recv()
            rim_heads(g)

        @pl.when(s == 0)
        def _():
            sum_images()
        @pl.when(s == 2)
        def _():
            gather_px()
            cube_send(0)
        for step in range(1, len(bits)):
            @pl.when(s == 2 + step)
            def _():
                cube_wait(step - 1)
                cube_send(step)
        @pl.when(s == 2 + len(bits))
        def _():
            cube_wait(len(bits) - 1)
            finish_grads()
        return carry

    lax.fori_loop(0, NG + 1, advance, 0)

    def drain(g, carry):
        for side in range(2):
            @pl.when(has_x[side])
            def _():
                z_copy(side, g).wait_send()
            @pl.when(has_y[side])
            def _():
                for which in range(2):
                    y_copy(which, side, g, 1 - side).wait_send()
            for side_x in range(2):
                @pl.when(has_y[side] & has_x[side_x])
                def _():
                    c_copy(side, side_x, g, 1 - side).wait_send()
        return carry

    lax.fori_loop(0, NG, drain, 0)
    for h in range(HEADS):
        oy, ox = owner_of(h)
        @pl.when(jnp.logical_not((py == oy) & (px == ox)))
        def _():
            m_copy(h, me).wait_send()
    @pl.when(own)
    def _():
        for d in range(1, ni):
            x_copy(d).wait_send()
        for d in range(1, npx):
            g_copy(d, my_head).wait_send()
    for step in range(len(bits)):
        for r, slot in zip(held(step), slots(step)):
            h_copy(bits[step], r * per_py, per_py, slot).wait_send()


def per_device(sizes, queries, keys, values, pattern, targets, router_q, router_k):
    ni, npy, npx = sizes
    _, ty, tx, feat = queries.shape
    group = npy * npx
    dma = pltpu.SemaphoreType.DMA
    vmem = pl.BlockSpec(memory_space=pltpu.VMEM)
    smem = pl.BlockSpec(memory_space=pltpu.SMEM)
    attended, grad_q, grad_k = pl.pallas_call(
        functools.partial(kernel, sizes),
        out_shape=(
            jax.ShapeDtypeStruct((ty, tx, feat), BF16),
            jax.ShapeDtypeStruct((HEADS, DH, RW), F32),
            jax.ShapeDtypeStruct((HEADS, DH, RW), F32),
        ),
        in_specs=[vmem, vmem, vmem, smem, smem, vmem, vmem],
        out_specs=(vmem, vmem, vmem),
        scratch_shapes=[
            pltpu.VMEM((HEADS, 4 * BB, DH), BF16),
            pltpu.VMEM((2, NG, 2, 2 * BB, GL), BF16),
            pltpu.VMEM((2, NG, 2, 2 * BB, GL), BF16),
            pltpu.VMEM((2, NG, 2, BS, 2 * BS, GL), BF16),
            pltpu.VMEM((2, 2, NG, 2, BB, GL), BF16),
            pltpu.VMEM((HEADS, 4 * BB, DH), F32),
            pltpu.VMEM((HEADS, 4 * BB, DH), F32),
            pltpu.VMEM((HEADS, 4 * BB, DH), F32),
            pltpu.VMEM((4, BS, 4 * BB), F32),
            pltpu.VMEM((4, BS, 6 * BB), F32),
            pltpu.VMEM((HEADS, 16, DH), F32),
            pltpu.VMEM((group, 16, DH), F32),
            pltpu.VMEM((ni, DH, 2 * RW), F32),
            pltpu.VMEM((HEADS, DH, 2 * RW), BF16),
            dma((2, NG)), dma((2, NG)),
            dma((2, 2, NG)), dma((2, 2, NG)),
            dma((2, 2, NG)), dma((2, 2, NG)),
            dma((HEADS,)), dma((group,)),
            dma((ni,)), dma((ni,)),
            dma((npx,)), dma((HEADS,)),
            dma((npy,)), dma((npy,)),
        ],
        compiler_params=pltpu.CompilerParams(
            collective_id=0, has_side_effects=True, vmem_limit_bytes=48 * 2 ** 20
        ),
    )(queries[0], keys[0], values[0], pattern, targets, router_q, router_k)
    return attended[None], grad_q, grad_k


def solution(mesh):
    sizes = tuple(mesh.shape[a] for a in ("img", "py", "px"))
    return jax.shard_map(
        functools.partial(per_device, sizes),
        mesh=mesh,
        in_specs=(
            P("img", "py", "px", None),
            P("img", "py", "px", None),
            P("img", "py", "px", None),
            P("img", "py", "px", None),
            P("img", "py", "px", None, None),
            P(),
            P(),
        ),
        out_specs=(P("img", "py", "px", None), P(), P()),
        check_vma=False,
    )
```

```python
import functools
import math

import jax
import jax.numpy as jnp
from jax import lax
from jax.experimental import pallas as pl
from jax.experimental.pallas import tpu as pltpu
from jax.sharding import PartitionSpec as P

HEADS = 12
DH = 128
RW = 64
BS = 8
TOPK = 3
NOFF = 9
HG = 2
NG = HEADS // HG
GL = HG * DH
WINDOW = 4
BB = BS * BS
DEAD = -1e30
LIVE = 3e38
MESH = pl.DeviceIdType.MESH
F32 = jnp.float32
BF16 = jnp.bfloat16
HIGH = lax.Precision.HIGHEST


def lanes(start, size):
    return pl.ds(pl.multiple_of(start, DH), size)


def tile_blocks(x):
    return [x[by * BS:(by + 1) * BS, bx * BS:(bx + 1) * BS] for by in range(2) for bx in range(2)]


def dot_t(a, b):
    return lax.dot_general(a, b, (((1,), (1,)), ((), ())), preferred_element_type=F32)


def kernel(
    sizes, q_in, k_in, v_in, pat_ref, tgt_ref, wq_in, wk_in,
    out_hbm, g_hbm,
    q_ref, k_ref, v_ref, wq_s, wk_s, out_ref,
    q_s, zs, zr, yr, cr, acc, den, top, cap_a, cap_b, msg, pool, xbuf, gbuf,
    zs_sem, zr_sem, ys_sem, yr_sem, cs_sem, cr_sem,
    ms_sem, mr_sem, xs_sem, xr_sem, gs_sem, gr_sem, hs_sem, hr_sem, in_sem, out_sem,
):
    ni, npy, npx = sizes
    per_py = HEADS // npy
    group = npy * npx
    img = lax.axis_index("img")
    py = lax.axis_index("py")
    px = lax.axis_index("px")
    me = py * npx + px
    has_x = (px > 0, px < npx - 1)
    has_y = (py > 0, py < npy - 1)
    to_x = (px - 1, px + 1)
    to_y = (py - 1, py + 1)

    barrier = pltpu.get_barrier_semaphore()
    for d in range(1, group):
        other = lax.rem(me + d, group)
        pl.semaphore_signal(
            barrier, inc=1,
            device_id={"py": lax.div(other, npx), "px": lax.rem(other, npx)},
            device_id_type=MESH,
        )
    for d in range(1, ni):
        pl.semaphore_signal(
            barrier, inc=1, device_id={"img": lax.rem(img + d, ni)}, device_id_type=MESH
        )

    loads = [
        pltpu.make_async_copy(a, b, in_sem.at[i])
        for i, (a, b) in enumerate(((q_in, q_ref), (k_in, k_ref), (v_in, v_ref)))
    ]
    for load in loads:
        load.start()
    turn = lax.rem(px + npx * HEADS - py * per_py, npx)
    own = turn < per_py
    my_head = jnp.minimum(py * per_py + turn, HEADS - 1)
    weights = [
        pltpu.make_async_copy(wq_in.at[my_head], wq_s, in_sem.at[3]),
        pltpu.make_async_copy(wk_in.at[my_head], wk_s, in_sem.at[4]),
    ]
    for load in weights:
        load.start()

    def z_copy(side, g):
        return pltpu.make_async_remote_copy(
            src_ref=zs.at[side, g], dst_ref=zr.at[1 - side, g],
            send_sem=zs_sem.at[side, g], recv_sem=zr_sem.at[1 - side, g],
            device_id={"px": to_x[side]}, device_id_type=MESH,
        )

    def z_arrival(side, g):
        return pltpu.make_async_remote_copy(
            src_ref=zs.at[side, g], dst_ref=zr.at[side, g],
            send_sem=zs_sem.at[side, g], recv_sem=zr_sem.at[side, g],
            device_id={"px": to_x[side]}, device_id_type=MESH,
        )

    def y_rows(which, side, g):
        ref = (k_ref, v_ref)[which]
        return ref.at[pl.ds(side * BS, BS), :, lanes(g * GL, GL)]

    def y_copy(which, side, g, slot):
        return pltpu.make_async_remote_copy(
            src_ref=y_rows(which, side, g), dst_ref=yr.at[slot, g, which],
            send_sem=ys_sem.at[side, which, g], recv_sem=yr_sem.at[slot, which, g],
            device_id={"py": to_y[side]}, device_id_type=MESH,
        )

    def c_copy(side_y, side_x, g, slot):
        return pltpu.make_async_remote_copy(
            src_ref=zr.at[side_x, g, :, pl.ds(side_y * BB, BB)],
            dst_ref=cr.at[slot, side_x, g],
            send_sem=cs_sem.at[side_y, side_x, g], recv_sem=cr_sem.at[slot, side_x, g],
            device_id={"py": to_y[side_y]}, device_id_type=MESH,
        )

    def send_z(g):
        for side in range(2):
            @pl.when(has_x[side])
            def _():
                z_copy(side, g).start()

    def send_y(g):
        for side in range(2):
            @pl.when(has_y[side])
            def _():
                for which in range(2):
                    y_copy(which, side, g, 1 - side).start()

    def cap_of(block, dy, dx):
        by, bx = divmod(block, 2)
        off = (dy + 1) * 3 + dx + 1
        return jnp.where(pat_ref[0, by, bx, off] > 0, F32(LIVE), F32(DEAD))

    lane_a = lax.broadcasted_iota(jnp.int32, (BS, 4 * BB), 1)
    lane_b = lax.broadcasted_iota(jnp.int32, (BS, 2 * BB), 1)
    for block in range(4):
        by, bx = divmod(block, 2)
        sy, sx = 2 * by - 1, 2 * bx - 1
        col_a = lax.rem(lax.div(lane_a, BS), 2)
        col_b = lax.rem(lax.div(lane_b, BS), 2)

        def pick(row, col, a, b):
            return jnp.where(col > 0, b, a)

        rows = [
            jnp.where(col_a > 0, cap_of(block, r - by, 1 - bx), cap_of(block, r - by, -bx))
            for r in range(2)
        ]
        cap_a[block] = jnp.where(lane_a >= 2 * BB, rows[1], rows[0])
        cap_b[block, :, 0:128] = jnp.where(
            lane_b >= BB, cap_of(block, 1 - by, sx), cap_of(block, -by, sx)
        )
        cap_b[block, :, 128:256] = jnp.where(
            col_b > 0, cap_of(block, sy, 1 - bx), cap_of(block, sy, -bx)
        )
        corner = cap_of(block, sy, sx)
        if bx == 0:
            cap_b[block, :, 256:384] = jnp.where(lane_b >= BB, F32(DEAD), corner)
        else:
            cap_b[block, :, 256:384] = jnp.where(lane_b >= BB, corner, F32(DEAD))

    def prepare(g, carry):
        for j in range(HG):
            h = g * HG + j
            hl = lanes(h * DH, DH)
            jl = pl.ds(j * DH, DH)
            q = q_ref[:, :, hl].astype(F32)
            k = k_ref[:, :, hl].astype(F32)
            v = v_ref[:, :, hl].astype(F32)
            parts = tile_blocks(q)
            q_s[h] = jnp.concatenate([b.reshape(BB, DH) for b in parts], axis=0).astype(BF16)
            for b in range(4):
                msg[h, b:b + 1, :] = jnp.sum(
                    jnp.sum(parts[b], axis=0), axis=0, keepdims=True) / BB
            parts = tile_blocks(k)
            for b in range(4):
                msg[h, 4 + b:5 + b, :] = jnp.sum(
                    jnp.sum(parts[b], axis=0), axis=0, keepdims=True) / BB
            for side in range(2):
                sl = slice(side * BS, (side + 1) * BS)
                zs[side, g, 0, :, jl] = k[:, sl, :].reshape(2 * BB, DH).astype(BF16)
                zs[side, g, 1, :, jl] = v[:, sl, :].reshape(2 * BB, DH).astype(BF16)
        return carry

    lane = lax.broadcasted_iota(jnp.int32, (1, DH), 1)
    code_rows = []
    for block in range(4):
        by, bx = divmod(block, 2)
        row = jnp.full((1, DH), -1.0, F32)
        for o in range(NOFF):
            row = jnp.where(
                lane == o, jnp.where(pat_ref[0, by, bx, o] > 0, F32(0.0), F32(-1.0)), row)
        code_rows.append(row)

    def encode(h, carry):
        for block in range(4):
            by, bx = divmod(block, 2)
            chosen = lane == tgt_ref[0, by, 0, bx, h]
            for t in range(1, TOPK):
                chosen = chosen | (lane == tgt_ref[0, by, t, bx, h])
            row = jnp.where(code_rows[block] < 0, F32(-1.0), jnp.where(chosen, F32(1.0), F32(0.0)))
            msg[h, 8 + block:9 + block, :] = row
        msg[h, 12:16, :] = jnp.zeros((4, DH), F32)
        return carry

    lax.fori_loop(0, HEADS, encode, 0)

    for load in loads:
        load.wait()
    lax.fori_loop(0, NG, prepare, 0)

    for side in range(2):
        @pl.when(jnp.logical_not(has_x[side]))
        def _():
            zr[side] = jnp.zeros(zr.shape[1:], BF16)
        @pl.when(jnp.logical_not(has_y[side]))
        def _():
            yr[side] = jnp.zeros(yr.shape[1:], BF16)
        for other in range(2):
            @pl.when(jnp.logical_not(has_y[side] & has_x[other]))
            def _():
                cr[side, other] = jnp.zeros(cr.shape[2:], BF16)

    pl.semaphore_wait(barrier, group - 1 + ni - 1)
    send_z(0)

    def owner_of(h):
        return h // per_py, h % npx

    def m_copy(h, slot):
        oy, ox = owner_of(h)
        return pltpu.make_async_remote_copy(
            src_ref=msg.at[h], dst_ref=pool.at[slot],
            send_sem=ms_sem.at[h], recv_sem=mr_sem.at[slot],
            device_id={"py": oy, "px": ox}, device_id_type=MESH,
        )

    for h in range(HEADS):
        oy, ox = owner_of(h)
        @pl.when(jnp.logical_not((py == oy) & (px == ox)))
        def _():
            m_copy(h, me).start()

    send_y(0)
    for g in range(1, WINDOW):
        send_z(g)
        send_y(g)

    scale = math.log2(math.e) / math.sqrt(DH)
    ones = jnp.ones((2 * DH, DH), BF16)

    def local_heads(g, carry):
        for j in range(HG):
            h = g * HG + j
            hl = lanes(h * DH, DH)
            key = k_ref[:, :, hl].reshape(4 * BB, DH)
            val = v_ref[:, :, hl].reshape(4 * BB, DH)
            s = dot_t(q_s[h], key)
            s = jnp.minimum(s.reshape(4, BS, BS, 4 * BB), cap_a[...][:, None]).reshape(4 * BB, 4 * BB)
            m = jnp.max(s, axis=-1, keepdims=True)
            p = jnp.exp2((s - m) * scale).astype(BF16)
            r = jnp.dot(p, jnp.concatenate([val, ones], axis=1), preferred_element_type=F32)
            acc[h] = r[:, :DH]
            den[h] = r[:, DH:]
            top[h] = jnp.broadcast_to(m, (4 * BB, DH))
        return carry

    lax.fori_loop(0, NG // 2, local_heads, 0)

    def x_copy(d):
        return pltpu.make_async_remote_copy(
            src_ref=xbuf.at[img], dst_ref=xbuf.at[img],
            send_sem=xs_sem.at[d], recv_sem=xr_sem.at[d],
            device_id={"img": lax.rem(img + d, ni)}, device_id_type=MESH,
        )

    def x_arrival(d):
        src = lax.rem(img + ni - d, ni)
        return pltpu.make_async_remote_copy(
            src_ref=xbuf.at[src], dst_ref=xbuf.at[src],
            send_sem=xs_sem.at[d], recv_sem=xr_sem.at[d],
            device_id={"img": lax.rem(img + d, ni)}, device_id_type=MESH,
        )

    for load in weights:
        load.wait()

    @pl.when(own)
    def _():
        pool[me] = msg[my_head]
        for src in range(group):
            @pl.when(me != src)
            def _():
                m_copy(0, src).wait_recv()
        nb = 4 * group
        pq = jnp.concatenate([pool[s, 0:4, :] for s in range(group)], axis=0)
        pk = jnp.concatenate([pool[s, 4:8, :] for s in range(group)], axis=0)
        code = jnp.concatenate([pool[s, 8:12, :] for s in range(group)], axis=0)
        rq, rk = [
            lax.dot_general(
                a, w[...], (((1,), (1,)), ((), ())), precision=HIGH, preferred_element_type=F32)
            for a, w in ((pq, wq_s), (pk, wk_s))
        ]
        logits = lax.dot_general(
            rq, rk, (((1,), (1,)), ((), ())), precision=HIGH, preferred_element_type=F32
        ) / math.sqrt(RW)

        def place(i):
            s = lax.div(i, 4)
            b = lax.rem(i, 4)
            return (
                lax.div(s, npx) * 2 + lax.div(b, 2),
                lax.rem(s, npx) * 2 + lax.rem(b, 2),
            )

        iy, ix = place(lax.broadcasted_iota(jnp.int32, (nb, nb), 0))
        jy, jx = place(lax.broadcasted_iota(jnp.int32, (nb, nb), 1))
        picks = jnp.full((nb, nb), -1.0, F32)
        for o in range(NOFF):
            dy, dx = o // 3 - 1, o % 3 - 1
            picks = jnp.where((jy - iy == dy) & (jx - ix == dx), code[:, o:o + 1], picks)
        live = picks >= 0
        logits = jnp.where(live, logits, DEAD)
        e = jnp.where(live, jnp.exp(logits - jnp.max(logits, axis=-1, keepdims=True)), 0.0)
        prob = e / jnp.sum(e, axis=-1, keepdims=True)
        picks = jnp.where(live, picks, 0.0)
        count = jnp.sum(picks, axis=-1, keepdims=True)
        normal = float(TOPK * HEADS * nb) * math.sqrt(RW)
        dl = jnp.where(live, count * prob - picks, 0.0) / normal
        drq = jnp.dot(dl, rk, precision=HIGH, preferred_element_type=F32)
        drk = lax.dot_general(
            dl, rq, (((0,), (0,)), ((), ())), precision=HIGH, preferred_element_type=F32)
        grads = [
            lax.dot_general(
                a, b, (((0,), (0,)), ((), ())), precision=HIGH, preferred_element_type=F32)
            for a, b in ((drq, pq), (drk, pk))
        ]
        xbuf[img] = jnp.concatenate(grads, axis=0)
        for d in range(1, ni):
            x_copy(d).start()

    lax.fori_loop(NG // 2, NG, local_heads, 0)

    def g_copy(d, head):
        return pltpu.make_async_remote_copy(
            src_ref=gbuf.at[head], dst_ref=gbuf.at[head],
            send_sem=gs_sem.at[d], recv_sem=gr_sem.at[head],
            device_id={"px": lax.rem(px + d, npx)}, device_id_type=MESH,
        )

    def sum_images():
        @pl.when(own)
        def _():
            for d in range(1, ni):
                x_arrival(d).wait_recv()
            total = xbuf[0]
            for i in range(1, ni):
                total = total + xbuf[i]
            gbuf[my_head] = total.astype(BF16)
            for d in range(1, npx):
                g_copy(d, my_head).start()

    def h_copy(bit, start, count, slot):
        mate = py + bit - 2 * bit * lax.rem(lax.div(py, bit), 2)
        return pltpu.make_async_remote_copy(
            src_ref=gbuf.at[pl.ds(start, count)], dst_ref=gbuf.at[pl.ds(start, count)],
            send_sem=hs_sem.at[slot], recv_sem=hr_sem.at[slot],
            device_id={"py": mate}, device_id_type=MESH,
        )

    bits = []
    b = npy // 2
    while b:
        bits.append(b)
        b //= 2

    def held(step):
        found = [py]
        for s in range(step):
            bit = bits[s]
            found = found + [r + bit - 2 * bit * lax.rem(lax.div(r, bit), 2) for r in found]
        return found

    def slots(step):
        return [2 ** step - 1 + i for i in range(2 ** step)]

    def cube_send(step):
        for r, slot in zip(held(step), slots(step)):
            h_copy(bits[step], r * per_py, per_py, slot).start()

    def cube_wait(step):
        bit = bits[step]
        for r, slot in zip(held(step), slots(step)):
            other = r + bit - 2 * bit * lax.rem(lax.div(r, bit), 2)
            h_copy(bit, other * per_py, per_py, slot).wait_recv()

    def gather_px():
        for i in range(per_py):
            head = py * per_py + i
            @pl.when(jnp.logical_not(own & (my_head == head)))
            def _():
                g_copy(1, head).wait_recv()

    def finish_grads():
        pltpu.make_async_copy(gbuf, g_hbm, out_sem.at[NG]).start()

    def rim_heads(g):
        for j in range(HG):
            h = g * HG + j
            jl = pl.ds(j * DH, DH)
            q = q_s[h]
            qb = [q[i * BB:(i + 1) * BB] for i in range(4)]
            sx, sy, vx, vy = [], [], [], []
            for side in range(2):
                key = zr[side, g, 0, :, jl]
                sx.append(dot_t(jnp.concatenate([qb[side], qb[2 + side]], axis=0), key))
                vx.append(jnp.concatenate([zr[side, g, 1, :, jl], ones[:2 * BB]], axis=1))
                key = jnp.concatenate(
                    [yr[side, g, 0, :, :, jl].reshape(2 * BB, DH),
                     cr[side, 0, g, 0, :, jl], cr[side, 1, g, 0, :, jl]], axis=0)
                val = jnp.concatenate(
                    [yr[side, g, 1, :, :, jl].reshape(2 * BB, DH),
                     cr[side, 0, g, 1, :, jl], cr[side, 1, g, 1, :, jl]], axis=0)
                sy.append(dot_t(q[side * 2 * BB:(side + 1) * 2 * BB], key))
                vy.append(jnp.concatenate([val, ones], axis=1))
            wx, wy, ms = [], [], []
            for i in range(4):
                by, bx = divmod(i, 2)
                a = sx[bx][by * BB:(by + 1) * BB].reshape(BS, BS, 2 * BB)
                c = sy[by][bx * BB:(bx + 1) * BB].reshape(BS, BS, 4 * BB)
                a = jnp.minimum(a, cap_b[i, :, 0:2 * BB][None]).reshape(BB, 2 * BB)
                c = jnp.minimum(c, cap_b[i, :, 2 * BB:6 * BB][None]).reshape(BB, 4 * BB)
                widest = jnp.maximum(a, jnp.maximum(c[:, :2 * BB], c[:, 2 * BB:]))
                m = jnp.maximum(
                    top[h, i * BB:(i + 1) * BB, :], jnp.max(widest, axis=-1, keepdims=True))
                wx.append(jnp.exp2((a - m) * scale).astype(BF16))
                wy.append(jnp.exp2((c - jnp.concatenate([m, m], axis=1)) * scale).astype(BF16))
                ms.append(m)
            rx = [
                jnp.dot(jnp.concatenate([wx[s], wx[2 + s]], axis=0), vx[s],
                        preferred_element_type=F32)
                for s in range(2)
            ]
            ry = [
                jnp.dot(jnp.concatenate([wy[2 * s], wy[2 * s + 1]], axis=0), vy[s],
                        preferred_element_type=F32)
                for s in range(2)
            ]
            outs = []
            for i in range(4):
                by, bx = divmod(i, 2)
                rows = slice(i * BB, (i + 1) * BB)
                old = jnp.exp2((top[h, rows, :] - ms[i]) * scale)
                r = rx[bx][by * BB:(by + 1) * BB] + ry[by][bx * BB:(bx + 1) * BB]
                num = acc[h, rows, :] * old + r[:, :DH]
                tot = den[h, rows, :] * old + r[:, DH:]
                outs.append((num / tot).reshape(BS, BS, DH))
            for by in range(2):
                out_ref[by * BS:(by + 1) * BS, :, lanes(h * DH, DH)] = jnp.concatenate(
                    [outs[2 * by], outs[2 * by + 1]], axis=1).astype(BF16)
        out_copy(g).start()

    def out_copy(g):
        gl = lanes(g * GL, GL)
        return pltpu.make_async_copy(
            out_ref.at[:, :, gl], out_hbm.at[:, :, gl], out_sem.at[g])

    def advance(s, carry):
        @pl.when(s < NG)
        def _():
            for side in range(2):
                @pl.when(has_x[side])
                def _():
                    z_arrival(side, s).wait_recv()
                for side_y in range(2):
                    @pl.when(has_x[side] & has_y[side_y])
                    def _():
                        c_copy(side_y, side, s, 1 - side_y).start()

            @pl.when(s + WINDOW < NG)
            def _():
                send_z(s + WINDOW)
                send_y(s + WINDOW)

        @pl.when(s >= 1)
        def _():
            g = s - 1
            for side in range(2):
                @pl.when(has_y[side])
                def _():
                    for which in range(2):
                        y_copy(which, side, g, side).wait_recv()
                for side_x in range(2):
                    @pl.when(has_y[side] & has_x[side_x])
                    def _():
                        c_copy(side, side_x, g, side).wait_recv()
            rim_heads(g)

        @pl.when(s == 1)
        def _():
            sum_images()
        @pl.when(s == 3)
        def _():
            gather_px()
            cube_send(0)
        for step in range(1, len(bits)):
            @pl.when(s == 3 + step)
            def _():
                cube_wait(step - 1)
                cube_send(step)
        @pl.when(s == 3 + len(bits))
        def _():
            cube_wait(len(bits) - 1)
            finish_grads()
        return carry

    lax.fori_loop(0, NG + 1, advance, 0)

    def drain(g, carry):
        for side in range(2):
            @pl.when(has_x[side])
            def _():
                z_copy(side, g).wait_send()
            @pl.when(has_y[side])
            def _():
                for which in range(2):
                    y_copy(which, side, g, 1 - side).wait_send()
            for side_x in range(2):
                @pl.when(has_y[side] & has_x[side_x])
                def _():
                    c_copy(side, side_x, g, 1 - side).wait_send()
        out_copy(g).wait()
        return carry

    lax.fori_loop(0, NG, drain, 0)
    pltpu.make_async_copy(gbuf, g_hbm, out_sem.at[NG]).wait()
    for h in range(HEADS):
        oy, ox = owner_of(h)
        @pl.when(jnp.logical_not((py == oy) & (px == ox)))
        def _():
            m_copy(h, me).wait_send()
    @pl.when(own)
    def _():
        for d in range(1, ni):
            x_copy(d).wait_send()
        for d in range(1, npx):
            g_copy(d, my_head).wait_send()
    for step in range(len(bits)):
        for r, slot in zip(held(step), slots(step)):
            h_copy(bits[step], r * per_py, per_py, slot).wait_send()


def per_device(sizes, queries, keys, values, pattern, targets, router_q, router_k):
    ni, npy, npx = sizes
    _, ty, tx, feat = queries.shape
    group = npy * npx
    dma = pltpu.SemaphoreType.DMA
    away = pl.BlockSpec(memory_space=pl.ANY)
    smem = pl.BlockSpec(memory_space=pltpu.SMEM)
    attended, grads = pl.pallas_call(
        functools.partial(kernel, sizes),
        out_shape=(
            jax.ShapeDtypeStruct((ty, tx, feat), BF16),
            jax.ShapeDtypeStruct((HEADS, 2 * RW, DH), BF16),
        ),
        in_specs=[away, away, away, smem, smem, away, away],
        out_specs=(away, away),
        scratch_shapes=[
            pltpu.VMEM((ty, tx, feat), BF16),
            pltpu.VMEM((ty, tx, feat), BF16),
            pltpu.VMEM((ty, tx, feat), BF16),
            pltpu.VMEM((RW, DH), F32),
            pltpu.VMEM((RW, DH), F32),
            pltpu.VMEM((ty, tx, feat), BF16),
            pltpu.VMEM((HEADS, 4 * BB, DH), BF16),
            pltpu.VMEM((2, NG, 2, 2 * BB, GL), BF16),
            pltpu.VMEM((2, NG, 2, 2 * BB, GL), BF16),
            pltpu.VMEM((2, NG, 2, BS, 2 * BS, GL), BF16),
            pltpu.VMEM((2, 2, NG, 2, BB, GL), BF16),
            pltpu.VMEM((HEADS, 4 * BB, DH), F32),
            pltpu.VMEM((HEADS, 4 * BB, DH), F32),
            pltpu.VMEM((HEADS, 4 * BB, DH), F32),
            pltpu.VMEM((4, BS, 4 * BB), F32),
            pltpu.VMEM((4, BS, 6 * BB), F32),
            pltpu.VMEM((HEADS, 16, DH), F32),
            pltpu.VMEM((group, 16, DH), F32),
            pltpu.VMEM((ni, 2 * RW, DH), F32),
            pltpu.VMEM((HEADS, 2 * RW, DH), BF16),
            dma((2, NG)), dma((2, NG)),
            dma((2, 2, NG)), dma((2, 2, NG)),
            dma((2, 2, NG)), dma((2, 2, NG)),
            dma((HEADS,)), dma((group,)),
            dma((ni,)), dma((ni,)),
            dma((npx,)), dma((HEADS,)),
            dma((npy,)), dma((npy,)), dma((5,)), dma((NG + 1,)),
        ],
        compiler_params=pltpu.CompilerParams(
            collective_id=0, has_side_effects=True, vmem_limit_bytes=56 * 2 ** 20
        ),
    )(
        queries[0], keys[0], values[0], pattern, jnp.transpose(targets, (0, 1, 4, 2, 3)),
        jnp.swapaxes(router_q, 1, 2), jnp.swapaxes(router_k, 1, 2),
    )
    grad_q, grad_k = [
        jnp.swapaxes(grads[:, i * RW:(i + 1) * RW].astype(F32), 1, 2) for i in range(2)]
    return attended[None], grad_q, grad_k


def solution(mesh):
    sizes = tuple(mesh.shape[a] for a in ("img", "py", "px"))
    return jax.shard_map(
        functools.partial(per_device, sizes),
        mesh=mesh,
        in_specs=(
            P("img", "py", "px", None),
            P("img", "py", "px", None),
            P("img", "py", "px", None),
            P("img", "py", "px", None),
            P("img", "py", "px", None, None),
            P(),
            P(),
        ),
        out_specs=(P("img", "py", "px", None), P(), P()),
        check_vma=False,
    )
```

```python
import functools
import math

import jax
import jax.numpy as jnp
from jax import lax
from jax.experimental import pallas as pl
from jax.experimental.pallas import tpu as pltpu
from jax.sharding import PartitionSpec as P

HEADS = 12
DH = 128
RW = 64
BS = 8
TOPK = 3
NOFF = 9
HG = 2
NG = HEADS // HG
GL = HG * DH
WINDOW = 4
BB = BS * BS
DEAD = -1e30
LIVE = 3e38
MESH = pl.DeviceIdType.MESH
F32 = jnp.float32
BF16 = jnp.bfloat16
HIGH = lax.Precision.HIGHEST


def lanes(start, size):
    return pl.ds(pl.multiple_of(start, DH), size)


def tile_blocks(x):
    return [x[by * BS:(by + 1) * BS, bx * BS:(bx + 1) * BS] for by in range(2) for bx in range(2)]


def dot_t(a, b):
    return lax.dot_general(a, b, (((1,), (1,)), ((), ())), preferred_element_type=F32)


def kernel(
    sizes, q_in, k_in, v_in, pat_ref, tgt_ref, wq_in, wk_in,
    out_hbm, gq_hbm, gk_hbm,
    q_ref, k_ref, v_ref, wq_s, wk_s, out_ref, gq_s, gk_s,
    q_s, zs, zr, yr, cr, acc, den, top, cap_a, cap_b, msg, pool, xbuf, gbuf,
    zs_sem, zr_sem, ys_sem, yr_sem, cs_sem, cr_sem,
    ms_sem, mr_sem, xs_sem, xr_sem, gs_sem, gr_sem, hs_sem, hr_sem, in_sem, out_sem,
):
    ni, npy, npx = sizes
    per_py = HEADS // npy
    group = npy * npx
    img = lax.axis_index("img")
    py = lax.axis_index("py")
    px = lax.axis_index("px")
    me = py * npx + px
    has_x = (px > 0, px < npx - 1)
    has_y = (py > 0, py < npy - 1)
    to_x = (px - 1, px + 1)
    to_y = (py - 1, py + 1)

    barrier = pltpu.get_barrier_semaphore()
    for d in range(1, group):
        other = lax.rem(me + d, group)
        pl.semaphore_signal(
            barrier, inc=1,
            device_id={"py": lax.div(other, npx), "px": lax.rem(other, npx)},
            device_id_type=MESH,
        )
    for d in range(1, ni):
        pl.semaphore_signal(
            barrier, inc=1, device_id={"img": lax.rem(img + d, ni)}, device_id_type=MESH
        )

    loads = [
        pltpu.make_async_copy(a, b, in_sem.at[i])
        for i, (a, b) in enumerate(((k_in, k_ref), (v_in, v_ref), (q_in, q_ref)))
    ]
    for load in loads:
        load.start()
    turn = lax.rem(px + npx * HEADS - py * per_py, npx)
    own = turn < per_py
    my_head = jnp.minimum(py * per_py + turn, HEADS - 1)
    weights = [
        pltpu.make_async_copy(wq_in.at[my_head], wq_s, in_sem.at[3]),
        pltpu.make_async_copy(wk_in.at[my_head], wk_s, in_sem.at[4]),
    ]
    for load in weights:
        load.start()

    def z_copy(side, g):
        return pltpu.make_async_remote_copy(
            src_ref=zs.at[side, g], dst_ref=zr.at[1 - side, g],
            send_sem=zs_sem.at[side, g], recv_sem=zr_sem.at[1 - side, g],
            device_id={"px": to_x[side]}, device_id_type=MESH,
        )

    def z_arrival(side, g):
        return pltpu.make_async_remote_copy(
            src_ref=zs.at[side, g], dst_ref=zr.at[side, g],
            send_sem=zs_sem.at[side, g], recv_sem=zr_sem.at[side, g],
            device_id={"px": to_x[side]}, device_id_type=MESH,
        )

    def y_rows(which, side, g):
        ref = (k_ref, v_ref)[which]
        return ref.at[pl.ds(side * BS, BS), :, lanes(g * GL, GL)]

    def y_copy(which, side, g, slot):
        return pltpu.make_async_remote_copy(
            src_ref=y_rows(which, side, g), dst_ref=yr.at[slot, g, which],
            send_sem=ys_sem.at[side, which, g], recv_sem=yr_sem.at[slot, which, g],
            device_id={"py": to_y[side]}, device_id_type=MESH,
        )

    def c_copy(side_y, side_x, g, slot):
        return pltpu.make_async_remote_copy(
            src_ref=zr.at[side_x, g, :, pl.ds(side_y * BB, BB)],
            dst_ref=cr.at[slot, side_x, g],
            send_sem=cs_sem.at[side_y, side_x, g], recv_sem=cr_sem.at[slot, side_x, g],
            device_id={"py": to_y[side_y]}, device_id_type=MESH,
        )

    def send_z(g):
        for side in range(2):
            @pl.when(has_x[side])
            def _():
                z_copy(side, g).start()

    def send_y(g):
        for side in range(2):
            @pl.when(has_y[side])
            def _():
                for which in range(2):
                    y_copy(which, side, g, 1 - side).start()

    def cap_of(block, dy, dx):
        by, bx = divmod(block, 2)
        off = (dy + 1) * 3 + dx + 1
        return jnp.where(pat_ref[0, by, bx, off] > 0, F32(LIVE), F32(DEAD))

    lane_a = lax.broadcasted_iota(jnp.int32, (BS, 4 * BB), 1)
    lane_b = lax.broadcasted_iota(jnp.int32, (BS, 2 * BB), 1)
    for block in range(4):
        by, bx = divmod(block, 2)
        sy, sx = 2 * by - 1, 2 * bx - 1
        col_a = lax.rem(lax.div(lane_a, BS), 2)
        col_b = lax.rem(lax.div(lane_b, BS), 2)

        def pick(row, col, a, b):
            return jnp.where(col > 0, b, a)

        rows = [
            jnp.where(col_a > 0, cap_of(block, r - by, 1 - bx), cap_of(block, r - by, -bx))
            for r in range(2)
        ]
        cap_a[block] = jnp.where(lane_a >= 2 * BB, rows[1], rows[0])
        cap_b[block, :, 0:128] = jnp.where(
            lane_b >= BB, cap_of(block, 1 - by, sx), cap_of(block, -by, sx)
        )
        cap_b[block, :, 128:256] = jnp.where(
            col_b > 0, cap_of(block, sy, 1 - bx), cap_of(block, sy, -bx)
        )
        corner = cap_of(block, sy, sx)
        if bx == 0:
            cap_b[block, :, 256:384] = jnp.where(lane_b >= BB, F32(DEAD), corner)
        else:
            cap_b[block, :, 256:384] = jnp.where(lane_b >= BB, corner, F32(DEAD))

    lane = lax.broadcasted_iota(jnp.int32, (1, DH), 1)
    code_rows = []
    for block in range(4):
        by, bx = divmod(block, 2)
        row = jnp.full((1, DH), -1.0, F32)
        for o in range(NOFF):
            row = jnp.where(
                lane == o, jnp.where(pat_ref[0, by, bx, o] > 0, F32(0.0), F32(-1.0)), row)
        code_rows.append(row)

    def encode(h, carry):
        for block in range(4):
            by, bx = divmod(block, 2)
            chosen = lane == tgt_ref[0, by, 0, bx, h]
            for t in range(1, TOPK):
                chosen = chosen | (lane == tgt_ref[0, by, t, bx, h])
            row = jnp.where(code_rows[block] < 0, F32(-1.0), jnp.where(chosen, F32(1.0), F32(0.0)))
            msg[h, 8 + block:9 + block, :] = row
        msg[h, 12:16, :] = jnp.zeros((4, DH), F32)
        return carry

    lax.fori_loop(0, HEADS, encode, 0)

    def pack(g):
        for which, ref in enumerate((k_ref, v_ref)):
            x = ref[:, :, lanes(g * GL, GL)].astype(F32)
            for side in range(2):
                zs[side, g, which] = x[:, side * BS:(side + 1) * BS, :].reshape(
                    2 * BB, GL).astype(BF16)

    def prepare(g, carry):
        for j in range(HG):
            h = g * HG + j
            hl = lanes(h * DH, DH)
            for at, ref in enumerate((q_ref, k_ref)):
                parts = tile_blocks(ref[:, :, hl].astype(F32))
                if at == 0:
                    q_s[h] = jnp.concatenate(
                        [b.reshape(BB, DH) for b in parts], axis=0).astype(BF16)
                for b in range(4):
                    msg[h, 4 * at + b:4 * at + b + 1, :] = jnp.sum(
                        jnp.sum(parts[b], axis=0), axis=0, keepdims=True) / BB
        return carry

    loads[0].wait()
    loads[1].wait()
    pack(0)
    pl.semaphore_wait(barrier, group - 1 + ni - 1)
    send_z(0)
    send_y(0)
    loads[2].wait()
    lax.fori_loop(0, NG, prepare, 0)

    def owner_of(h):
        return h // per_py, h % npx

    def m_copy(h, slot):
        oy, ox = owner_of(h)
        return pltpu.make_async_remote_copy(
            src_ref=msg.at[h], dst_ref=pool.at[slot],
            send_sem=ms_sem.at[h], recv_sem=mr_sem.at[slot],
            device_id={"py": oy, "px": ox}, device_id_type=MESH,
        )

    for h in range(HEADS):
        oy, ox = owner_of(h)
        @pl.when(jnp.logical_not((py == oy) & (px == ox)))
        def _():
            m_copy(h, me).start()

    def pack_and_send(g, carry):
        pack(g)

        @pl.when(g < WINDOW)
        def _():
            send_z(g)
            send_y(g)
        return carry

    lax.fori_loop(1, NG, pack_and_send, 0)

    for side in range(2):
        @pl.when(jnp.logical_not(has_x[side]))
        def _():
            zr[side] = jnp.zeros(zr.shape[1:], BF16)
        @pl.when(jnp.logical_not(has_y[side]))
        def _():
            yr[side] = jnp.zeros(yr.shape[1:], BF16)
        for other in range(2):
            @pl.when(jnp.logical_not(has_y[side] & has_x[other]))
            def _():
                cr[side, other] = jnp.zeros(cr.shape[2:], BF16)


    scale = math.log2(math.e) / math.sqrt(DH)
    ones = jnp.ones((2 * DH, DH), BF16)

    def local_heads(g, carry):
        for j in range(HG):
            h = g * HG + j
            hl = lanes(h * DH, DH)
            key = k_ref[:, :, hl].reshape(4 * BB, DH)
            val = v_ref[:, :, hl].reshape(4 * BB, DH)
            s = dot_t(q_s[h], key)
            s = jnp.minimum(s.reshape(4, BS, BS, 4 * BB), cap_a[...][:, None]).reshape(4 * BB, 4 * BB)
            m = jnp.max(s, axis=-1, keepdims=True)
            p = jnp.exp2((s - m) * scale).astype(BF16)
            r = jnp.dot(p, jnp.concatenate([val, ones], axis=1), preferred_element_type=F32)
            acc[h] = r[:, :DH]
            den[h] = r[:, DH:]
            top[h] = jnp.broadcast_to(m, (4 * BB, DH))
        return carry

    def forward(s):
        for side in range(2):
            @pl.when(has_x[side])
            def _():
                z_arrival(side, s).wait_recv()
            for side_y in range(2):
                @pl.when(has_x[side] & has_y[side_y])
                def _():
                    c_copy(side_y, side, s, 1 - side_y).start()

        @pl.when(s + WINDOW < NG)
        def _():
            send_z(s + WINDOW)
            send_y(s + WINDOW)

    lax.fori_loop(0, NG // 2, local_heads, 0)
    forward(0)
    lax.fori_loop(NG // 2, NG, local_heads, 0)
    forward(1)

    def x_copy(d):
        return pltpu.make_async_remote_copy(
            src_ref=xbuf.at[img], dst_ref=xbuf.at[img],
            send_sem=xs_sem.at[d], recv_sem=xr_sem.at[d],
            device_id={"img": lax.rem(img + d, ni)}, device_id_type=MESH,
        )

    def x_arrival(d):
        src = lax.rem(img + ni - d, ni)
        return pltpu.make_async_remote_copy(
            src_ref=xbuf.at[src], dst_ref=xbuf.at[src],
            send_sem=xs_sem.at[d], recv_sem=xr_sem.at[d],
            device_id={"img": lax.rem(img + d, ni)}, device_id_type=MESH,
        )

    for load in weights:
        load.wait()

    @pl.when(own)
    def _():
        pool[me] = msg[my_head]
        for src in range(group):
            @pl.when(me != src)
            def _():
                m_copy(0, src).wait_recv()
        nb = 4 * group
        pq = jnp.concatenate([pool[s, 0:4, :] for s in range(group)], axis=0)
        pk = jnp.concatenate([pool[s, 4:8, :] for s in range(group)], axis=0)
        code = jnp.concatenate([pool[s, 8:12, :] for s in range(group)], axis=0)
        rq, rk = [
            lax.dot_general(
                a, w[...], (((1,), (1,)), ((), ())), precision=HIGH, preferred_element_type=F32)
            for a, w in ((pq, wq_s), (pk, wk_s))
        ]
        logits = lax.dot_general(
            rq, rk, (((1,), (1,)), ((), ())), precision=HIGH, preferred_element_type=F32
        ) / math.sqrt(RW)

        def place(i):
            s = lax.div(i, 4)
            b = lax.rem(i, 4)
            return (
                lax.div(s, npx) * 2 + lax.div(b, 2),
                lax.rem(s, npx) * 2 + lax.rem(b, 2),
            )

        iy, ix = place(lax.broadcasted_iota(jnp.int32, (nb, nb), 0))
        jy, jx = place(lax.broadcasted_iota(jnp.int32, (nb, nb), 1))
        picks = jnp.full((nb, nb), -1.0, F32)
        for o in range(NOFF):
            dy, dx = o // 3 - 1, o % 3 - 1
            picks = jnp.where((jy - iy == dy) & (jx - ix == dx), code[:, o:o + 1], picks)
        live = picks >= 0
        logits = jnp.where(live, logits, DEAD)
        e = jnp.where(live, jnp.exp(logits - jnp.max(logits, axis=-1, keepdims=True)), 0.0)
        prob = e / jnp.sum(e, axis=-1, keepdims=True)
        picks = jnp.where(live, picks, 0.0)
        count = jnp.sum(picks, axis=-1, keepdims=True)
        normal = float(TOPK * HEADS * nb) * math.sqrt(RW)
        dl = jnp.where(live, count * prob - picks, 0.0) / normal
        drq = jnp.dot(dl, rk, precision=HIGH, preferred_element_type=F32)
        drk = lax.dot_general(
            dl, rq, (((0,), (0,)), ((), ())), precision=HIGH, preferred_element_type=F32)
        grads = [
            lax.dot_general(
                a, b, (((0,), (0,)), ((), ())), precision=HIGH, preferred_element_type=F32)
            for a, b in ((drq, pq), (drk, pk))
        ]
        xbuf[img] = jnp.concatenate(grads, axis=0)
        for d in range(1, ni):
            x_copy(d).start()

    def g_copy(d, head):
        return pltpu.make_async_remote_copy(
            src_ref=gbuf.at[head], dst_ref=gbuf.at[head],
            send_sem=gs_sem.at[d], recv_sem=gr_sem.at[head],
            device_id={"px": lax.rem(px + d, npx)}, device_id_type=MESH,
        )

    def sum_images():
        @pl.when(own)
        def _():
            for d in range(1, ni):
                x_arrival(d).wait_recv()
            total = xbuf[0]
            for i in range(1, ni):
                total = total + xbuf[i]
            gbuf[my_head] = total.astype(BF16)
            for d in range(1, npx):
                g_copy(d, my_head).start()

    def h_copy(bit, start, count, slot):
        mate = py + bit - 2 * bit * lax.rem(lax.div(py, bit), 2)
        return pltpu.make_async_remote_copy(
            src_ref=gbuf.at[pl.ds(start, count)], dst_ref=gbuf.at[pl.ds(start, count)],
            send_sem=hs_sem.at[slot], recv_sem=hr_sem.at[slot],
            device_id={"py": mate}, device_id_type=MESH,
        )

    bits = []
    b = npy // 2
    while b:
        bits.append(b)
        b //= 2

    def held(step):
        found = [py]
        for s in range(step):
            bit = bits[s]
            found = found + [r + bit - 2 * bit * lax.rem(lax.div(r, bit), 2) for r in found]
        return found

    def slots(step):
        return [2 ** step - 1 + i for i in range(2 ** step)]

    def cube_send(step):
        for r, slot in zip(held(step), slots(step)):
            h_copy(bits[step], r * per_py, per_py, slot).start()

    def cube_wait(step):
        bit = bits[step]
        for r, slot in zip(held(step), slots(step)):
            other = r + bit - 2 * bit * lax.rem(lax.div(r, bit), 2)
            h_copy(bit, other * per_py, per_py, slot).wait_recv()

    def gather_px():
        for i in range(per_py):
            head = py * per_py + i
            @pl.when(jnp.logical_not(own & (my_head == head)))
            def _():
                g_copy(1, head).wait_recv()

    def finish_grads():
        def widen(h, carry):
            gq_s[h] = gbuf[h, 0:RW, :].astype(F32)
            gk_s[h] = gbuf[h, RW:2 * RW, :].astype(F32)
            return carry

        lax.fori_loop(0, HEADS, widen, 0)
        for store in grad_copies():
            store.start()

    def grad_copies():
        return [
            pltpu.make_async_copy(gq_s, gq_hbm, out_sem.at[NG]),
            pltpu.make_async_copy(gk_s, gk_hbm, out_sem.at[NG + 1]),
        ]

    def rim_heads(g):
        for j in range(HG):
            h = g * HG + j
            jl = pl.ds(j * DH, DH)
            q = q_s[h]
            qb = [q[i * BB:(i + 1) * BB] for i in range(4)]
            sx, sy, vx, vy = [], [], [], []
            for side in range(2):
                key = zr[side, g, 0, :, jl]
                sx.append(dot_t(jnp.concatenate([qb[side], qb[2 + side]], axis=0), key))
                vx.append(jnp.concatenate([zr[side, g, 1, :, jl], ones[:2 * BB]], axis=1))
                key = jnp.concatenate(
                    [yr[side, g, 0, :, :, jl].reshape(2 * BB, DH),
                     cr[side, 0, g, 0, :, jl], cr[side, 1, g, 0, :, jl]], axis=0)
                val = jnp.concatenate(
                    [yr[side, g, 1, :, :, jl].reshape(2 * BB, DH),
                     cr[side, 0, g, 1, :, jl], cr[side, 1, g, 1, :, jl]], axis=0)
                sy.append(dot_t(q[side * 2 * BB:(side + 1) * 2 * BB], key))
                vy.append(jnp.concatenate([val, ones], axis=1))
            wx, wy, ms = [], [], []
            for i in range(4):
                by, bx = divmod(i, 2)
                a = sx[bx][by * BB:(by + 1) * BB].reshape(BS, BS, 2 * BB)
                c = sy[by][bx * BB:(bx + 1) * BB].reshape(BS, BS, 4 * BB)
                a = jnp.minimum(a, cap_b[i, :, 0:2 * BB][None]).reshape(BB, 2 * BB)
                c = jnp.minimum(c, cap_b[i, :, 2 * BB:6 * BB][None]).reshape(BB, 4 * BB)
                widest = jnp.maximum(a, jnp.maximum(c[:, :2 * BB], c[:, 2 * BB:]))
                m = jnp.maximum(
                    top[h, i * BB:(i + 1) * BB, :], jnp.max(widest, axis=-1, keepdims=True))
                wx.append(jnp.exp2((a - m) * scale).astype(BF16))
                wy.append(jnp.exp2((c - jnp.concatenate([m, m], axis=1)) * scale).astype(BF16))
                ms.append(m)
            rx = [
                jnp.dot(jnp.concatenate([wx[s], wx[2 + s]], axis=0), vx[s],
                        preferred_element_type=F32)
                for s in range(2)
            ]
            ry = [
                jnp.dot(jnp.concatenate([wy[2 * s], wy[2 * s + 1]], axis=0), vy[s],
                        preferred_element_type=F32)
                for s in range(2)
            ]
            outs = []
            for i in range(4):
                by, bx = divmod(i, 2)
                rows = slice(i * BB, (i + 1) * BB)
                old = jnp.exp2((top[h, rows, :] - ms[i]) * scale)
                r = rx[bx][by * BB:(by + 1) * BB] + ry[by][bx * BB:(bx + 1) * BB]
                num = acc[h, rows, :] * old + r[:, :DH]
                tot = den[h, rows, :] * old + r[:, DH:]
                outs.append((num / tot).reshape(BS, BS, DH))
            for by in range(2):
                out_ref[by * BS:(by + 1) * BS, :, lanes(h * DH, DH)] = jnp.concatenate(
                    [outs[2 * by], outs[2 * by + 1]], axis=1).astype(BF16)
        out_copy(g).start()

    def out_copy(g):
        gl = lanes(g * GL, GL)
        return pltpu.make_async_copy(
            out_ref.at[:, :, gl], out_hbm.at[:, :, gl], out_sem.at[g])

    def advance(s, carry):
        @pl.when((s >= 2) & (s < NG))
        def _():
            forward(s)

        g = s - 1
        for side in range(2):
            @pl.when(has_y[side])
            def _():
                for which in range(2):
                    y_copy(which, side, g, side).wait_recv()
            for side_x in range(2):
                @pl.when(has_y[side] & has_x[side_x])
                def _():
                    c_copy(side, side_x, g, side).wait_recv()
        rim_heads(g)

        @pl.when(s == 1)
        def _():
            sum_images()
        @pl.when(s == 3)
        def _():
            gather_px()
            cube_send(0)
        for step in range(1, len(bits)):
            @pl.when(s == 3 + step)
            def _():
                cube_wait(step - 1)
                cube_send(step)
        @pl.when(s == 3 + len(bits))
        def _():
            cube_wait(len(bits) - 1)
            finish_grads()
        return carry

    lax.fori_loop(1, NG + 1, advance, 0)

    def drain(g, carry):
        for side in range(2):
            @pl.when(has_x[side])
            def _():
                z_copy(side, g).wait_send()
            @pl.when(has_y[side])
            def _():
                for which in range(2):
                    y_copy(which, side, g, 1 - side).wait_send()
            for side_x in range(2):
                @pl.when(has_y[side] & has_x[side_x])
                def _():
                    c_copy(side, side_x, g, 1 - side).wait_send()
        out_copy(g).wait()
        return carry

    lax.fori_loop(0, NG, drain, 0)
    for store in grad_copies():
        store.wait()
    for h in range(HEADS):
        oy, ox = owner_of(h)
        @pl.when(jnp.logical_not((py == oy) & (px == ox)))
        def _():
            m_copy(h, me).wait_send()
    @pl.when(own)
    def _():
        for d in range(1, ni):
            x_copy(d).wait_send()
        for d in range(1, npx):
            g_copy(d, my_head).wait_send()
    for step in range(len(bits)):
        for r, slot in zip(held(step), slots(step)):
            h_copy(bits[step], r * per_py, per_py, slot).wait_send()


def per_device(sizes, queries, keys, values, pattern, targets, router_q, router_k):
    ni, npy, npx = sizes
    _, ty, tx, feat = queries.shape
    group = npy * npx
    dma = pltpu.SemaphoreType.DMA
    away = pl.BlockSpec(memory_space=pl.ANY)
    smem = pl.BlockSpec(memory_space=pltpu.SMEM)
    attended, grad_q, grad_k = pl.pallas_call(
        functools.partial(kernel, sizes),
        out_shape=(
            jax.ShapeDtypeStruct((ty, tx, feat), BF16),
            jax.ShapeDtypeStruct((HEADS, RW, DH), F32),
            jax.ShapeDtypeStruct((HEADS, RW, DH), F32),
        ),
        in_specs=[away, away, away, smem, smem, away, away],
        out_specs=(away, away, away),
        scratch_shapes=[
            pltpu.VMEM((ty, tx, feat), BF16),
            pltpu.VMEM((ty, tx, feat), BF16),
            pltpu.VMEM((ty, tx, feat), BF16),
            pltpu.VMEM((RW, DH), F32),
            pltpu.VMEM((RW, DH), F32),
            pltpu.VMEM((ty, tx, feat), BF16),
            pltpu.VMEM((HEADS, RW, DH), F32),
            pltpu.VMEM((HEADS, RW, DH), F32),
            pltpu.VMEM((HEADS, 4 * BB, DH), BF16),
            pltpu.VMEM((2, NG, 2, 2 * BB, GL), BF16),
            pltpu.VMEM((2, NG, 2, 2 * BB, GL), BF16),
            pltpu.VMEM((2, NG, 2, BS, 2 * BS, GL), BF16),
            pltpu.VMEM((2, 2, NG, 2, BB, GL), BF16),
            pltpu.VMEM((HEADS, 4 * BB, DH), F32),
            pltpu.VMEM((HEADS, 4 * BB, DH), F32),
            pltpu.VMEM((HEADS, 4 * BB, DH), F32),
            pltpu.VMEM((4, BS, 4 * BB), F32),
            pltpu.VMEM((4, BS, 6 * BB), F32),
            pltpu.VMEM((HEADS, 16, DH), F32),
            pltpu.VMEM((group, 16, DH), F32),
            pltpu.VMEM((ni, 2 * RW, DH), F32),
            pltpu.VMEM((HEADS, 2 * RW, DH), BF16),
            dma((2, NG)), dma((2, NG)),
            dma((2, 2, NG)), dma((2, 2, NG)),
            dma((2, 2, NG)), dma((2, 2, NG)),
            dma((HEADS,)), dma((group,)),
            dma((ni,)), dma((ni,)),
            dma((npx,)), dma((HEADS,)),
            dma((npy,)), dma((npy,)), dma((5,)), dma((NG + 2,)),
        ],
        compiler_params=pltpu.CompilerParams(
            collective_id=0, has_side_effects=True, vmem_limit_bytes=56 * 2 ** 20
        ),
    )(
        queries[0], keys[0], values[0], pattern, jnp.transpose(targets, (0, 1, 4, 2, 3)),
        jnp.swapaxes(router_q, 1, 2), jnp.swapaxes(router_k, 1, 2),
    )
    return attended[None], jnp.swapaxes(grad_q, 1, 2), jnp.swapaxes(grad_k, 1, 2)


def solution(mesh):
    sizes = tuple(mesh.shape[a] for a in ("img", "py", "px"))
    return jax.shard_map(
        functools.partial(per_device, sizes),
        mesh=mesh,
        in_specs=(
            P("img", "py", "px", None),
            P("img", "py", "px", None),
            P("img", "py", "px", None),
            P("img", "py", "px", None),
            P("img", "py", "px", None, None),
            P(),
            P(),
        ),
        out_specs=(P("img", "py", "px", None), P(), P()),
        check_vma=False,
    )
```

```python
import functools
import math

import jax
import jax.numpy as jnp
from jax import lax
from jax.experimental import pallas as pl
from jax.experimental.pallas import tpu as pltpu
from jax.sharding import PartitionSpec as P

HEADS = 12
DH = 128
RW = 64
BS = 8
TOPK = 3
NOFF = 9
HG = 3
NG = HEADS // HG
GL = HG * DH
WINDOW = 3
BB = BS * BS
DEAD = -1e30
LIVE = 3e38
MESH = pl.DeviceIdType.MESH
F32 = jnp.float32
BF16 = jnp.bfloat16
HIGH = lax.Precision.HIGHEST


def lanes(start, size):
    return pl.ds(pl.multiple_of(start, DH), size)


def tile_blocks(x):
    return [x[by * BS:(by + 1) * BS, bx * BS:(bx + 1) * BS] for by in range(2) for bx in range(2)]


def dot_t(a, b):
    return lax.dot_general(a, b, (((1,), (1,)), ((), ())), preferred_element_type=F32)


def kernel(
    sizes, q_in, k_in, v_in, pat_ref, tgt_ref, wq_in, wk_in,
    out_hbm, gq_hbm, gk_hbm,
    q_ref, k_ref, v_ref, wq_s, wk_s, out_ref, gq_s, gk_s,
    q_s, zs, zr, yr, cr, acc, den, top, cap_a, cap_b, msg, pool, xbuf, gbuf,
    zs_sem, zr_sem, ys_sem, yr_sem, cs_sem, cr_sem,
    ms_sem, mr_sem, xs_sem, xr_sem, gs_sem, gr_sem, hs_sem, hr_sem, in_sem, out_sem,
):
    ni, npy, npx = sizes
    per_py = HEADS // npy
    group = npy * npx
    img = lax.axis_index("img")
    py = lax.axis_index("py")
    px = lax.axis_index("px")
    me = py * npx + px
    has_x = (px > 0, px < npx - 1)
    has_y = (py > 0, py < npy - 1)
    to_x = (px - 1, px + 1)
    to_y = (py - 1, py + 1)

    barrier = pltpu.get_barrier_semaphore()
    for d in range(1, group):
        other = lax.rem(me + d, group)
        pl.semaphore_signal(
            barrier, inc=1,
            device_id={"py": lax.div(other, npx), "px": lax.rem(other, npx)},
            device_id_type=MESH,
        )
    for d in range(1, ni):
        pl.semaphore_signal(
            barrier, inc=1, device_id={"img": lax.rem(img + d, ni)}, device_id_type=MESH
        )

    loads = [
        pltpu.make_async_copy(a, b, in_sem.at[i])
        for i, (a, b) in enumerate(((k_in, k_ref), (v_in, v_ref), (q_in, q_ref)))
    ]
    for load in loads:
        load.start()
    turn = lax.rem(px + npx * HEADS - py * per_py, npx)
    own = turn < per_py
    my_head = jnp.minimum(py * per_py + turn, HEADS - 1)
    weights = [
        pltpu.make_async_copy(wq_in.at[my_head], wq_s, in_sem.at[3]),
        pltpu.make_async_copy(wk_in.at[my_head], wk_s, in_sem.at[4]),
    ]
    for load in weights:
        load.start()

    def z_copy(side, g):
        return pltpu.make_async_remote_copy(
            src_ref=zs.at[side, g], dst_ref=zr.at[1 - side, g],
            send_sem=zs_sem.at[side, g], recv_sem=zr_sem.at[1 - side, g],
            device_id={"px": to_x[side]}, device_id_type=MESH,
        )

    def z_arrival(side, g):
        return pltpu.make_async_remote_copy(
            src_ref=zs.at[side, g], dst_ref=zr.at[side, g],
            send_sem=zs_sem.at[side, g], recv_sem=zr_sem.at[side, g],
            device_id={"px": to_x[side]}, device_id_type=MESH,
        )

    def y_rows(which, side, g):
        ref = (k_ref, v_ref)[which]
        return ref.at[pl.ds(side * BS, BS), :, lanes(g * GL, GL)]

    def y_copy(which, side, g, slot):
        return pltpu.make_async_remote_copy(
            src_ref=y_rows(which, side, g), dst_ref=yr.at[slot, g, which],
            send_sem=ys_sem.at[side, which, g], recv_sem=yr_sem.at[slot, which, g],
            device_id={"py": to_y[side]}, device_id_type=MESH,
        )

    def c_copy(side_y, side_x, g, slot):
        return pltpu.make_async_remote_copy(
            src_ref=zr.at[side_x, g, :, pl.ds(side_y * BB, BB)],
            dst_ref=cr.at[slot, side_x, g],
            send_sem=cs_sem.at[side_y, side_x, g], recv_sem=cr_sem.at[slot, side_x, g],
            device_id={"py": to_y[side_y]}, device_id_type=MESH,
        )

    def send_z(g):
        for side in range(2):
            @pl.when(has_x[side])
            def _():
                z_copy(side, g).start()

    def send_y(g):
        for side in range(2):
            @pl.when(has_y[side])
            def _():
                for which in range(2):
                    y_copy(which, side, g, 1 - side).start()

    def cap_of(block, dy, dx):
        by, bx = divmod(block, 2)
        off = (dy + 1) * 3 + dx + 1
        return jnp.where(pat_ref[0, by, bx, off] > 0, F32(LIVE), F32(DEAD))

    lane_a = lax.broadcasted_iota(jnp.int32, (BS, 4 * BB), 1)
    lane_b = lax.broadcasted_iota(jnp.int32, (BS, 2 * BB), 1)
    for block in range(4):
        by, bx = divmod(block, 2)
        sy, sx = 2 * by - 1, 2 * bx - 1
        col_a = lax.rem(lax.div(lane_a, BS), 2)
        col_b = lax.rem(lax.div(lane_b, BS), 2)

        def pick(row, col, a, b):
            return jnp.where(col > 0, b, a)

        rows = [
            jnp.where(col_a > 0, cap_of(block, r - by, 1 - bx), cap_of(block, r - by, -bx))
            for r in range(2)
        ]
        cap_a[block] = jnp.where(lane_a >= 2 * BB, rows[1], rows[0])
        cap_b[block, :, 0:128] = jnp.where(
            lane_b >= BB, cap_of(block, 1 - by, sx), cap_of(block, -by, sx)
        )
        cap_b[block, :, 128:256] = jnp.where(
            col_b > 0, cap_of(block, sy, 1 - bx), cap_of(block, sy, -bx)
        )
        corner = cap_of(block, sy, sx)
        if bx == 0:
            cap_b[block, :, 256:384] = jnp.where(lane_b >= BB, F32(DEAD), corner)
        else:
            cap_b[block, :, 256:384] = jnp.where(lane_b >= BB, corner, F32(DEAD))

    lane = lax.broadcasted_iota(jnp.int32, (1, DH), 1)
    code_rows = []
    for block in range(4):
        by, bx = divmod(block, 2)
        row = jnp.full((1, DH), -1.0, F32)
        for o in range(NOFF):
            row = jnp.where(
                lane == o, jnp.where(pat_ref[0, by, bx, o] > 0, F32(0.0), F32(-1.0)), row)
        code_rows.append(row)

    def encode(h, carry):
        for block in range(4):
            by, bx = divmod(block, 2)
            chosen = lane == tgt_ref[0, by, 0, bx, h]
            for t in range(1, TOPK):
                chosen = chosen | (lane == tgt_ref[0, by, t, bx, h])
            row = jnp.where(code_rows[block] < 0, F32(-1.0), jnp.where(chosen, F32(1.0), F32(0.0)))
            msg[h, 8 + block:9 + block, :] = row
        msg[h, 12:16, :] = jnp.zeros((4, DH), F32)
        return carry

    lax.fori_loop(0, HEADS, encode, 0)

    def pack(g):
        for which, ref in enumerate((k_ref, v_ref)):
            x = ref[:, :, lanes(g * GL, GL)].astype(F32)
            for side in range(2):
                zs[side, g, which] = x[:, side * BS:(side + 1) * BS, :].reshape(
                    2 * BB, GL).astype(BF16)

    def prepare(g, carry):
        for j in range(HG):
            h = g * HG + j
            hl = lanes(h * DH, DH)
            for at, ref in enumerate((q_ref, k_ref)):
                parts = tile_blocks(ref[:, :, hl].astype(F32))
                if at == 0:
                    q_s[h] = jnp.concatenate(
                        [b.reshape(BB, DH) for b in parts], axis=0).astype(BF16)
                for b in range(4):
                    msg[h, 4 * at + b:4 * at + b + 1, :] = jnp.sum(
                        jnp.sum(parts[b], axis=0), axis=0, keepdims=True) / BB
        return carry

    loads[0].wait()
    loads[1].wait()
    pack(0)
    pl.semaphore_wait(barrier, group - 1 + ni - 1)
    send_z(0)
    send_y(0)
    loads[2].wait()
    lax.fori_loop(0, NG, prepare, 0)

    def owner_of(h):
        return h // per_py, h % npx

    def m_copy(h, slot):
        oy, ox = owner_of(h)
        return pltpu.make_async_remote_copy(
            src_ref=msg.at[h], dst_ref=pool.at[slot],
            send_sem=ms_sem.at[h], recv_sem=mr_sem.at[slot],
            device_id={"py": oy, "px": ox}, device_id_type=MESH,
        )

    for h in range(HEADS):
        oy, ox = owner_of(h)
        @pl.when(jnp.logical_not((py == oy) & (px == ox)))
        def _():
            m_copy(h, me).start()

    def pack_and_send(g, carry):
        pack(g)

        @pl.when(g < WINDOW)
        def _():
            send_z(g)
            send_y(g)
        return carry

    lax.fori_loop(1, NG, pack_and_send, 0)

    for side in range(2):
        @pl.when(jnp.logical_not(has_x[side]))
        def _():
            zr[side] = jnp.zeros(zr.shape[1:], BF16)
        @pl.when(jnp.logical_not(has_y[side]))
        def _():
            yr[side] = jnp.zeros(yr.shape[1:], BF16)
        for other in range(2):
            @pl.when(jnp.logical_not(has_y[side] & has_x[other]))
            def _():
                cr[side, other] = jnp.zeros(cr.shape[2:], BF16)


    scale = math.log2(math.e) / math.sqrt(DH)
    ones = jnp.ones((2 * DH, DH), BF16)

    def local_heads(g, carry):
        for j in range(HG):
            h = g * HG + j
            hl = lanes(h * DH, DH)
            key = k_ref[:, :, hl].reshape(4 * BB, DH)
            val = v_ref[:, :, hl].reshape(4 * BB, DH)
            s = dot_t(q_s[h], key)
            s = jnp.minimum(s.reshape(4, BS, BS, 4 * BB), cap_a[...][:, None]).reshape(4 * BB, 4 * BB)
            m = jnp.max(s, axis=-1, keepdims=True)
            p = jnp.exp2((s - m) * scale).astype(BF16)
            r = jnp.dot(p, jnp.concatenate([val, ones], axis=1), preferred_element_type=F32)
            acc[h] = r[:, :DH]
            den[h] = r[:, DH:]
            top[h] = jnp.broadcast_to(m, (4 * BB, DH))
        return carry

    def forward(s):
        for side in range(2):
            @pl.when(has_x[side])
            def _():
                z_arrival(side, s).wait_recv()
            for side_y in range(2):
                @pl.when(has_x[side] & has_y[side_y])
                def _():
                    c_copy(side_y, side, s, 1 - side_y).start()

        @pl.when(s + WINDOW < NG)
        def _():
            send_z(s + WINDOW)
            send_y(s + WINDOW)

    lax.fori_loop(0, NG // 2, local_heads, 0, unroll=True)
    forward(0)
    lax.fori_loop(NG // 2, NG, local_heads, 0, unroll=True)
    forward(1)

    def x_copy(d):
        return pltpu.make_async_remote_copy(
            src_ref=xbuf.at[img], dst_ref=xbuf.at[img],
            send_sem=xs_sem.at[d], recv_sem=xr_sem.at[d],
            device_id={"img": lax.rem(img + d, ni)}, device_id_type=MESH,
        )

    def x_arrival(d):
        src = lax.rem(img + ni - d, ni)
        return pltpu.make_async_remote_copy(
            src_ref=xbuf.at[src], dst_ref=xbuf.at[src],
            send_sem=xs_sem.at[d], recv_sem=xr_sem.at[d],
            device_id={"img": lax.rem(img + d, ni)}, device_id_type=MESH,
        )

    for load in weights:
        load.wait()

    @pl.when(own)
    def _():
        pool[me] = msg[my_head]
        for src in range(group):
            @pl.when(me != src)
            def _():
                m_copy(0, src).wait_recv()
        nb = 4 * group
        pq = jnp.concatenate([pool[s, 0:4, :] for s in range(group)], axis=0)
        pk = jnp.concatenate([pool[s, 4:8, :] for s in range(group)], axis=0)
        code = jnp.concatenate([pool[s, 8:12, :] for s in range(group)], axis=0)
        rq, rk = [
            lax.dot_general(
                a, w[...], (((1,), (1,)), ((), ())), precision=HIGH, preferred_element_type=F32)
            for a, w in ((pq, wq_s), (pk, wk_s))
        ]
        logits = lax.dot_general(
            rq, rk, (((1,), (1,)), ((), ())), precision=HIGH, preferred_element_type=F32
        ) / math.sqrt(RW)

        def place(i):
            s = lax.div(i, 4)
            b = lax.rem(i, 4)
            return (
                lax.div(s, npx) * 2 + lax.div(b, 2),
                lax.rem(s, npx) * 2 + lax.rem(b, 2),
            )

        iy, ix = place(lax.broadcasted_iota(jnp.int32, (nb, nb), 0))
        jy, jx = place(lax.broadcasted_iota(jnp.int32, (nb, nb), 1))
        picks = jnp.full((nb, nb), -1.0, F32)
        for o in range(NOFF):
            dy, dx = o // 3 - 1, o % 3 - 1
            picks = jnp.where((jy - iy == dy) & (jx - ix == dx), code[:, o:o + 1], picks)
        live = picks >= 0
        logits = jnp.where(live, logits, DEAD)
        e = jnp.where(live, jnp.exp(logits - jnp.max(logits, axis=-1, keepdims=True)), 0.0)
        prob = e / jnp.sum(e, axis=-1, keepdims=True)
        picks = jnp.where(live, picks, 0.0)
        count = jnp.sum(picks, axis=-1, keepdims=True)
        normal = float(TOPK * HEADS * nb) * math.sqrt(RW)
        dl = jnp.where(live, count * prob - picks, 0.0) / normal
        drq = jnp.dot(dl, rk, precision=HIGH, preferred_element_type=F32)
        drk = lax.dot_general(
            dl, rq, (((0,), (0,)), ((), ())), precision=HIGH, preferred_element_type=F32)
        grads = [
            lax.dot_general(
                a, b, (((0,), (0,)), ((), ())), precision=HIGH, preferred_element_type=F32)
            for a, b in ((drq, pq), (drk, pk))
        ]
        xbuf[img] = jnp.concatenate(grads, axis=0)
        for d in range(1, ni):
            x_copy(d).start()

    def g_copy(d, head):
        return pltpu.make_async_remote_copy(
            src_ref=gbuf.at[head], dst_ref=gbuf.at[head],
            send_sem=gs_sem.at[d], recv_sem=gr_sem.at[head],
            device_id={"px": lax.rem(px + d, npx)}, device_id_type=MESH,
        )

    def sum_images():
        @pl.when(own)
        def _():
            for d in range(1, ni):
                x_arrival(d).wait_recv()
            total = xbuf[0]
            for i in range(1, ni):
                total = total + xbuf[i]
            gbuf[my_head] = total.astype(BF16)
            for d in range(1, npx):
                g_copy(d, my_head).start()

    def h_copy(bit, start, count, slot):
        mate = py + bit - 2 * bit * lax.rem(lax.div(py, bit), 2)
        return pltpu.make_async_remote_copy(
            src_ref=gbuf.at[pl.ds(start, count)], dst_ref=gbuf.at[pl.ds(start, count)],
            send_sem=hs_sem.at[slot], recv_sem=hr_sem.at[slot],
            device_id={"py": mate}, device_id_type=MESH,
        )

    bits = []
    b = npy // 2
    while b:
        bits.append(b)
        b //= 2

    def held(step):
        found = [py]
        for s in range(step):
            bit = bits[s]
            found = found + [r + bit - 2 * bit * lax.rem(lax.div(r, bit), 2) for r in found]
        return found

    def slots(step):
        return [2 ** step - 1 + i for i in range(2 ** step)]

    def cube_send(step):
        for r, slot in zip(held(step), slots(step)):
            h_copy(bits[step], r * per_py, per_py, slot).start()

    def cube_wait(step):
        bit = bits[step]
        for r, slot in zip(held(step), slots(step)):
            other = r + bit - 2 * bit * lax.rem(lax.div(r, bit), 2)
            h_copy(bit, other * per_py, per_py, slot).wait_recv()

    def gather_px():
        for i in range(per_py):
            head = py * per_py + i
            @pl.when(jnp.logical_not(own & (my_head == head)))
            def _():
                g_copy(1, head).wait_recv()

    def finish_grads():
        def widen(h, carry):
            gq_s[h] = gbuf[h, 0:RW, :].astype(F32)
            gk_s[h] = gbuf[h, RW:2 * RW, :].astype(F32)
            return carry

        lax.fori_loop(0, HEADS, widen, 0)
        for store in grad_copies():
            store.start()

    def grad_copies():
        return [
            pltpu.make_async_copy(gq_s, gq_hbm, out_sem.at[NG]),
            pltpu.make_async_copy(gk_s, gk_hbm, out_sem.at[NG + 1]),
        ]

    def rim_heads(g):
        for j in range(HG):
            h = g * HG + j
            jl = pl.ds(j * DH, DH)
            q = q_s[h]
            qb = [q[i * BB:(i + 1) * BB] for i in range(4)]
            sx, sy, vx, vy = [], [], [], []
            for side in range(2):
                key = zr[side, g, 0, :, jl]
                sx.append(dot_t(jnp.concatenate([qb[side], qb[2 + side]], axis=0), key))
                vx.append(jnp.concatenate([zr[side, g, 1, :, jl], ones[:2 * BB]], axis=1))
                key = jnp.concatenate(
                    [yr[side, g, 0, :, :, jl].reshape(2 * BB, DH),
                     cr[side, 0, g, 0, :, jl], cr[side, 1, g, 0, :, jl]], axis=0)
                val = jnp.concatenate(
                    [yr[side, g, 1, :, :, jl].reshape(2 * BB, DH),
                     cr[side, 0, g, 1, :, jl], cr[side, 1, g, 1, :, jl]], axis=0)
                sy.append(dot_t(q[side * 2 * BB:(side + 1) * 2 * BB], key))
                vy.append(jnp.concatenate([val, ones], axis=1))
            wx, wy, ms = [], [], []
            for i in range(4):
                by, bx = divmod(i, 2)
                a = sx[bx][by * BB:(by + 1) * BB].reshape(BS, BS, 2 * BB)
                c = sy[by][bx * BB:(bx + 1) * BB].reshape(BS, BS, 4 * BB)
                a = jnp.minimum(a, cap_b[i, :, 0:2 * BB][None]).reshape(BB, 2 * BB)
                c = jnp.minimum(c, cap_b[i, :, 2 * BB:6 * BB][None]).reshape(BB, 4 * BB)
                widest = jnp.maximum(a, jnp.maximum(c[:, :2 * BB], c[:, 2 * BB:]))
                m = jnp.maximum(
                    top[h, i * BB:(i + 1) * BB, :], jnp.max(widest, axis=-1, keepdims=True))
                wx.append(jnp.exp2((a - m) * scale).astype(BF16))
                wy.append(jnp.exp2((c - jnp.concatenate([m, m], axis=1)) * scale).astype(BF16))
                ms.append(m)
            rx = [
                jnp.dot(jnp.concatenate([wx[s], wx[2 + s]], axis=0), vx[s],
                        preferred_element_type=F32)
                for s in range(2)
            ]
            ry = [
                jnp.dot(jnp.concatenate([wy[2 * s], wy[2 * s + 1]], axis=0), vy[s],
                        preferred_element_type=F32)
                for s in range(2)
            ]
            outs = []
            for i in range(4):
                by, bx = divmod(i, 2)
                rows = slice(i * BB, (i + 1) * BB)
                old = jnp.exp2((top[h, rows, :] - ms[i]) * scale)
                r = rx[bx][by * BB:(by + 1) * BB] + ry[by][bx * BB:(bx + 1) * BB]
                num = acc[h, rows, :] * old + r[:, :DH]
                tot = den[h, rows, :] * old + r[:, DH:]
                outs.append((num / tot).reshape(BS, BS, DH))
            for by in range(2):
                out_ref[by * BS:(by + 1) * BS, :, lanes(h * DH, DH)] = jnp.concatenate(
                    [outs[2 * by], outs[2 * by + 1]], axis=1).astype(BF16)
        out_copy(g).start()

    def out_copy(g):
        gl = lanes(g * GL, GL)
        return pltpu.make_async_copy(
            out_ref.at[:, :, gl], out_hbm.at[:, :, gl], out_sem.at[g])

    def advance(s, carry):
        @pl.when((s >= 2) & (s < NG))
        def _():
            forward(s)

        g = s - 1
        for side in range(2):
            @pl.when(has_y[side])
            def _():
                for which in range(2):
                    y_copy(which, side, g, side).wait_recv()
            for side_x in range(2):
                @pl.when(has_y[side] & has_x[side_x])
                def _():
                    c_copy(side, side_x, g, side).wait_recv()
        rim_heads(g)

        @pl.when(s == 1)
        def _():
            sum_images()
        @pl.when(s == 2)
        def _():
            gather_px()
            cube_send(0)
        for step in range(1, len(bits)):
            @pl.when(s == 2 + step)
            def _():
                cube_wait(step - 1)
                cube_send(step)
        @pl.when(s == 2 + len(bits))
        def _():
            cube_wait(len(bits) - 1)
            finish_grads()
        return carry

    lax.fori_loop(1, NG + 1, advance, 0)

    def drain(g, carry):
        for side in range(2):
            @pl.when(has_x[side])
            def _():
                z_copy(side, g).wait_send()
            @pl.when(has_y[side])
            def _():
                for which in range(2):
                    y_copy(which, side, g, 1 - side).wait_send()
            for side_x in range(2):
                @pl.when(has_y[side] & has_x[side_x])
                def _():
                    c_copy(side, side_x, g, 1 - side).wait_send()
        out_copy(g).wait()
        return carry

    lax.fori_loop(0, NG, drain, 0)
    for store in grad_copies():
        store.wait()
    for h in range(HEADS):
        oy, ox = owner_of(h)
        @pl.when(jnp.logical_not((py == oy) & (px == ox)))
        def _():
            m_copy(h, me).wait_send()
    @pl.when(own)
    def _():
        for d in range(1, ni):
            x_copy(d).wait_send()
        for d in range(1, npx):
            g_copy(d, my_head).wait_send()
    for step in range(len(bits)):
        for r, slot in zip(held(step), slots(step)):
            h_copy(bits[step], r * per_py, per_py, slot).wait_send()


def hand_over(*refs):
    half = (len(refs) - 1) // 2
    sems = refs[-1]
    copies, at = [], 0
    for src, dst in zip(refs[:half], refs[half:-1]):
        step = src.shape[0] // 4
        for i in range(4):
            rows = pl.ds(i * step, step)
            copies.append(pltpu.make_async_copy(src.at[rows], dst.at[rows], sems.at[at]))
            at += 1
    for copy in copies:
        copy.start()
    for copy in copies:
        copy.wait()


def per_device(sizes, queries, keys, values, pattern, targets, router_q, router_k):
    ni, npy, npx = sizes
    _, ty, tx, feat = queries.shape
    group = npy * npx
    dma = pltpu.SemaphoreType.DMA
    away = pl.BlockSpec(memory_space=pl.ANY)
    smem = pl.BlockSpec(memory_space=pltpu.SMEM)
    attended, grad_q, grad_k = pl.pallas_call(
        functools.partial(kernel, sizes),
        out_shape=(
            jax.ShapeDtypeStruct((ty, tx, feat), BF16),
            jax.ShapeDtypeStruct((HEADS, RW, DH), F32),
            jax.ShapeDtypeStruct((HEADS, RW, DH), F32),
        ),
        in_specs=[away, away, away, smem, smem, away, away],
        out_specs=(away, away, away),
        scratch_shapes=[
            pltpu.VMEM((ty, tx, feat), BF16),
            pltpu.VMEM((ty, tx, feat), BF16),
            pltpu.VMEM((ty, tx, feat), BF16),
            pltpu.VMEM((RW, DH), F32),
            pltpu.VMEM((RW, DH), F32),
            pltpu.VMEM((ty, tx, feat), BF16),
            pltpu.VMEM((HEADS, RW, DH), F32),
            pltpu.VMEM((HEADS, RW, DH), F32),
            pltpu.VMEM((HEADS, 4 * BB, DH), BF16),
            pltpu.VMEM((2, NG, 2, 2 * BB, GL), BF16),
            pltpu.VMEM((2, NG, 2, 2 * BB, GL), BF16),
            pltpu.VMEM((2, NG, 2, BS, 2 * BS, GL), BF16),
            pltpu.VMEM((2, 2, NG, 2, BB, GL), BF16),
            pltpu.VMEM((HEADS, 4 * BB, DH), F32),
            pltpu.VMEM((HEADS, 4 * BB, DH), F32),
            pltpu.VMEM((HEADS, 4 * BB, DH), F32),
            pltpu.VMEM((4, BS, 4 * BB), F32),
            pltpu.VMEM((4, BS, 6 * BB), F32),
            pltpu.VMEM((HEADS, 16, DH), F32),
            pltpu.VMEM((group, 16, DH), F32),
            pltpu.VMEM((ni, 2 * RW, DH), F32),
            pltpu.VMEM((HEADS, 2 * RW, DH), BF16),
            dma((2, NG)), dma((2, NG)),
            dma((2, 2, NG)), dma((2, 2, NG)),
            dma((2, 2, NG)), dma((2, 2, NG)),
            dma((HEADS,)), dma((group,)),
            dma((ni,)), dma((ni,)),
            dma((npx,)), dma((HEADS,)),
            dma((npy,)), dma((npy,)), dma((5,)), dma((NG + 2,)),
        ],
        compiler_params=pltpu.CompilerParams(
            collective_id=0, has_side_effects=True, vmem_limit_bytes=56 * 2 ** 20
        ),
    )(
        queries[0], keys[0], values[0], pattern, jnp.transpose(targets, (0, 1, 4, 2, 3)),
        jnp.swapaxes(router_q, 1, 2), jnp.swapaxes(router_k, 1, 2),
    )
    made = (attended, grad_q, grad_k)
    attended, grad_q, grad_k = pl.pallas_call(
        hand_over,
        out_shape=tuple(jax.ShapeDtypeStruct(a.shape, a.dtype) for a in made),
        in_specs=[away] * 3,
        out_specs=(away,) * 3,
        scratch_shapes=[dma((12,))],
        compiler_params=pltpu.CompilerParams(vmem_limit_bytes=56 * 2 ** 20),
    )(*made)
    return attended[None], jnp.swapaxes(grad_q, 1, 2), jnp.swapaxes(grad_k, 1, 2)


def solution(mesh):
    sizes = tuple(mesh.shape[a] for a in ("img", "py", "px"))
    return jax.shard_map(
        functools.partial(per_device, sizes),
        mesh=mesh,
        in_specs=(
            P("img", "py", "px", None),
            P("img", "py", "px", None),
            P("img", "py", "px", None),
            P("img", "py", "px", None),
            P("img", "py", "px", None, None),
            P(),
            P(),
        ),
        out_specs=(P("img", "py", "px", None), P(), P()),
        check_vma=False,
    )
```

```python
import functools
import math

import jax
import jax.numpy as jnp
from jax import lax
from jax.experimental import pallas as pl
from jax.experimental.pallas import tpu as pltpu
from jax.sharding import PartitionSpec as P

HEADS = 12
DH = 128
RW = 64
BS = 8
TOPK = 3
NOFF = 9
HG = 3
NG = HEADS // HG
GL = HG * DH
WINDOW = 3
BB = BS * BS
DEAD = -1e30
LIVE = 3e38
MESH = pl.DeviceIdType.MESH
F32 = jnp.float32
BF16 = jnp.bfloat16
HIGH = lax.Precision.HIGHEST


def lanes(start, size):
    return pl.ds(pl.multiple_of(start, DH), size)


def tile_blocks(x):
    return [x[by * BS:(by + 1) * BS, bx * BS:(bx + 1) * BS] for by in range(2) for bx in range(2)]


def dot_t(a, b):
    return lax.dot_general(a, b, (((1,), (1,)), ((), ())), preferred_element_type=F32)


def kernel(
    sizes, q_in, k_in, v_in, pat_ref, tgt_ref, wq_in, wk_in,
    out_hbm, gq_hbm, gk_hbm,
    q_ref, k_ref, v_ref, wq_s, wk_s, out_ref, gq_s, gk_s,
    q_s, zs, zr, yr, cr, acc, den, top, cap_a, cap_b, msg, pool, xbuf, gbuf,
    zs_sem, zr_sem, ys_sem, yr_sem, cs_sem, cr_sem,
    ms_sem, mr_sem, xs_sem, xr_sem, gs_sem, gr_sem, hs_sem, hr_sem, in_sem, out_sem,
):
    ni, npy, npx = sizes
    per_py = HEADS // npy
    group = npy * npx
    img = lax.axis_index("img")
    py = lax.axis_index("py")
    px = lax.axis_index("px")
    me = py * npx + px
    has_x = (px > 0, px < npx - 1)
    has_y = (py > 0, py < npy - 1)
    to_x = (px - 1, px + 1)
    to_y = (py - 1, py + 1)

    barrier = pltpu.get_barrier_semaphore()
    for d in range(1, group):
        other = lax.rem(me + d, group)
        pl.semaphore_signal(
            barrier, inc=1,
            device_id={"py": lax.div(other, npx), "px": lax.rem(other, npx)},
            device_id_type=MESH,
        )
    for d in range(1, ni):
        pl.semaphore_signal(
            barrier, inc=1, device_id={"img": lax.rem(img + d, ni)}, device_id_type=MESH
        )

    loads = [
        pltpu.make_async_copy(a, b, in_sem.at[i])
        for i, (a, b) in enumerate(((k_in, k_ref), (v_in, v_ref), (q_in, q_ref)))
    ]
    for load in loads:
        load.start()
    turn = lax.rem(px + npx * HEADS - py * per_py, npx)
    own = turn < per_py
    my_head = jnp.minimum(py * per_py + turn, HEADS - 1)
    weights = [
        pltpu.make_async_copy(wq_in.at[my_head], wq_s, in_sem.at[3]),
        pltpu.make_async_copy(wk_in.at[my_head], wk_s, in_sem.at[4]),
    ]
    for load in weights:
        load.start()

    def z_copy(side, g):
        return pltpu.make_async_remote_copy(
            src_ref=zs.at[side, g], dst_ref=zr.at[1 - side, g],
            send_sem=zs_sem.at[side, g], recv_sem=zr_sem.at[1 - side, g],
            device_id={"px": to_x[side]}, device_id_type=MESH,
        )

    def z_arrival(side, g):
        return pltpu.make_async_remote_copy(
            src_ref=zs.at[side, g], dst_ref=zr.at[side, g],
            send_sem=zs_sem.at[side, g], recv_sem=zr_sem.at[side, g],
            device_id={"px": to_x[side]}, device_id_type=MESH,
        )

    def y_rows(which, side, g):
        ref = (k_ref, v_ref)[which]
        return ref.at[pl.ds(side * BS, BS), :, lanes(g * GL, GL)]

    def y_copy(which, side, g, slot):
        return pltpu.make_async_remote_copy(
            src_ref=y_rows(which, side, g), dst_ref=yr.at[slot, g, which],
            send_sem=ys_sem.at[side, which, g], recv_sem=yr_sem.at[slot, which, g],
            device_id={"py": to_y[side]}, device_id_type=MESH,
        )

    def c_copy(side_y, side_x, g, slot):
        return pltpu.make_async_remote_copy(
            src_ref=zr.at[side_x, g, :, pl.ds(side_y * BB, BB)],
            dst_ref=cr.at[slot, side_x, g],
            send_sem=cs_sem.at[side_y, side_x, g], recv_sem=cr_sem.at[slot, side_x, g],
            device_id={"py": to_y[side_y]}, device_id_type=MESH,
        )

    def send_z(g):
        for side in range(2):
            @pl.when(has_x[side])
            def _():
                z_copy(side, g).start()

    def send_y(g):
        for side in range(2):
            @pl.when(has_y[side])
            def _():
                for which in range(2):
                    y_copy(which, side, g, 1 - side).start()

    def cap_of(block, dy, dx):
        by, bx = divmod(block, 2)
        off = (dy + 1) * 3 + dx + 1
        return jnp.where(pat_ref[0, by, bx, off] > 0, F32(LIVE), F32(DEAD))

    lane_a = lax.broadcasted_iota(jnp.int32, (BS, 4 * BB), 1)
    lane_b = lax.broadcasted_iota(jnp.int32, (BS, 2 * BB), 1)
    for block in range(4):
        by, bx = divmod(block, 2)
        sy, sx = 2 * by - 1, 2 * bx - 1
        col_a = lax.rem(lax.div(lane_a, BS), 2)
        col_b = lax.rem(lax.div(lane_b, BS), 2)

        def pick(row, col, a, b):
            return jnp.where(col > 0, b, a)

        rows = [
            jnp.where(col_a > 0, cap_of(block, r - by, 1 - bx), cap_of(block, r - by, -bx))
            for r in range(2)
        ]
        cap_a[block] = jnp.where(lane_a >= 2 * BB, rows[1], rows[0])
        cap_b[block, :, 0:128] = jnp.where(
            lane_b >= BB, cap_of(block, 1 - by, sx), cap_of(block, -by, sx)
        )
        cap_b[block, :, 128:256] = jnp.where(
            col_b > 0, cap_of(block, sy, 1 - bx), cap_of(block, sy, -bx)
        )
        corner = cap_of(block, sy, sx)
        if bx == 0:
            cap_b[block, :, 256:384] = jnp.where(lane_b >= BB, F32(DEAD), corner)
        else:
            cap_b[block, :, 256:384] = jnp.where(lane_b >= BB, corner, F32(DEAD))

    lane = lax.broadcasted_iota(jnp.int32, (1, DH), 1)
    code_rows = []
    for block in range(4):
        by, bx = divmod(block, 2)
        row = jnp.full((1, DH), -1.0, F32)
        for o in range(NOFF):
            row = jnp.where(
                lane == o, jnp.where(pat_ref[0, by, bx, o] > 0, F32(0.0), F32(-1.0)), row)
        code_rows.append(row)

    def encode(h, carry):
        for block in range(4):
            by, bx = divmod(block, 2)
            chosen = lane == tgt_ref[0, by, 0, bx, h]
            for t in range(1, TOPK):
                chosen = chosen | (lane == tgt_ref[0, by, t, bx, h])
            row = jnp.where(code_rows[block] < 0, F32(-1.0), jnp.where(chosen, F32(1.0), F32(0.0)))
            msg[h, 8 + block:9 + block, :] = row
        msg[h, 12:16, :] = jnp.zeros((4, DH), F32)
        return carry

    lax.fori_loop(0, HEADS, encode, 0)

    def pack(g):
        for which, ref in enumerate((k_ref, v_ref)):
            x = ref[:, :, lanes(g * GL, GL)].astype(F32)
            for side in range(2):
                zs[side, g, which] = x[:, side * BS:(side + 1) * BS, :].reshape(
                    2 * BB, GL).astype(BF16)

    def prepare(g, carry):
        for j in range(HG):
            h = g * HG + j
            hl = lanes(h * DH, DH)
            for at, ref in enumerate((q_ref, k_ref)):
                parts = tile_blocks(ref[:, :, hl].astype(F32))
                if at == 0:
                    q_s[h] = jnp.concatenate(
                        [b.reshape(BB, DH) for b in parts], axis=0).astype(BF16)
                for b in range(4):
                    msg[h, 4 * at + b:4 * at + b + 1, :] = jnp.sum(
                        jnp.sum(parts[b], axis=0), axis=0, keepdims=True) / BB
        return carry

    loads[0].wait()
    loads[1].wait()
    pack(0)
    pl.semaphore_wait(barrier, group - 1 + ni - 1)
    send_z(0)
    send_y(0)
    loads[2].wait()
    lax.fori_loop(0, NG, prepare, 0)

    def owner_of(h):
        return h // per_py, h % npx

    def m_copy(h, slot):
        oy, ox = owner_of(h)
        return pltpu.make_async_remote_copy(
            src_ref=msg.at[h], dst_ref=pool.at[slot],
            send_sem=ms_sem.at[h], recv_sem=mr_sem.at[slot],
            device_id={"py": oy, "px": ox}, device_id_type=MESH,
        )

    for h in range(HEADS):
        oy, ox = owner_of(h)
        @pl.when(jnp.logical_not((py == oy) & (px == ox)))
        def _():
            m_copy(h, me).start()

    def pack_and_send(g, carry):
        pack(g)

        @pl.when(g < WINDOW)
        def _():
            send_z(g)
            send_y(g)
        return carry

    lax.fori_loop(1, NG, pack_and_send, 0)

    for side in range(2):
        @pl.when(jnp.logical_not(has_x[side]))
        def _():
            zr[side] = jnp.zeros(zr.shape[1:], BF16)
        @pl.when(jnp.logical_not(has_y[side]))
        def _():
            yr[side] = jnp.zeros(yr.shape[1:], BF16)
        for other in range(2):
            @pl.when(jnp.logical_not(has_y[side] & has_x[other]))
            def _():
                cr[side, other] = jnp.zeros(cr.shape[2:], BF16)


    scale = math.log2(math.e) / math.sqrt(DH)
    ones = jnp.ones((2 * DH, DH), BF16)

    def local_heads(g, carry):
        for j in range(HG):
            h = g * HG + j
            hl = lanes(h * DH, DH)
            key = k_ref[:, :, hl].reshape(4 * BB, DH)
            val = v_ref[:, :, hl].reshape(4 * BB, DH)
            s = dot_t(q_s[h], key)
            s = jnp.minimum(s.reshape(4, BS, BS, 4 * BB), cap_a[...][:, None]).reshape(4 * BB, 4 * BB)
            m = jnp.max(s, axis=-1, keepdims=True)
            p = jnp.exp2((s - m) * scale).astype(BF16)
            r = jnp.dot(p, jnp.concatenate([val, ones], axis=1), preferred_element_type=F32)
            acc[h] = r[:, :DH]
            den[h] = r[:, DH:]
            top[h] = jnp.broadcast_to(m, (4 * BB, DH))
        return carry

    def forward(s):
        for side in range(2):
            @pl.when(has_x[side])
            def _():
                z_arrival(side, s).wait_recv()
            for side_y in range(2):
                @pl.when(has_x[side] & has_y[side_y])
                def _():
                    c_copy(side_y, side, s, 1 - side_y).start()

        @pl.when(s + WINDOW < NG)
        def _():
            send_z(s + WINDOW)
            send_y(s + WINDOW)

    lax.fori_loop(0, NG // 2, local_heads, 0, unroll=True)
    forward(0)
    lax.fori_loop(NG // 2, NG, local_heads, 0, unroll=True)
    forward(1)

    def x_copy(d):
        return pltpu.make_async_remote_copy(
            src_ref=xbuf.at[img], dst_ref=xbuf.at[img],
            send_sem=xs_sem.at[d], recv_sem=xr_sem.at[d],
            device_id={"img": lax.rem(img + d, ni)}, device_id_type=MESH,
        )

    def x_arrival(d):
        src = lax.rem(img + ni - d, ni)
        return pltpu.make_async_remote_copy(
            src_ref=xbuf.at[src], dst_ref=xbuf.at[src],
            send_sem=xs_sem.at[d], recv_sem=xr_sem.at[d],
            device_id={"img": lax.rem(img + d, ni)}, device_id_type=MESH,
        )

    for load in weights:
        load.wait()

    @pl.when(own)
    def _():
        pool[me] = msg[my_head]
        for src in range(group):
            @pl.when(me != src)
            def _():
                m_copy(0, src).wait_recv()
        nb = 4 * group
        pq = jnp.concatenate([pool[s, 0:4, :] for s in range(group)], axis=0)
        pk = jnp.concatenate([pool[s, 4:8, :] for s in range(group)], axis=0)
        code = jnp.concatenate([pool[s, 8:12, :] for s in range(group)], axis=0)
        rq, rk = [
            lax.dot_general(
                a, w[...], (((1,), (1,)), ((), ())), precision=HIGH, preferred_element_type=F32)
            for a, w in ((pq, wq_s), (pk, wk_s))
        ]
        logits = lax.dot_general(
            rq, rk, (((1,), (1,)), ((), ())), precision=HIGH, preferred_element_type=F32
        ) / math.sqrt(RW)

        def place(i):
            s = lax.div(i, 4)
            b = lax.rem(i, 4)
            return (
                lax.div(s, npx) * 2 + lax.div(b, 2),
                lax.rem(s, npx) * 2 + lax.rem(b, 2),
            )

        iy, ix = place(lax.broadcasted_iota(jnp.int32, (nb, nb), 0))
        jy, jx = place(lax.broadcasted_iota(jnp.int32, (nb, nb), 1))
        picks = jnp.full((nb, nb), -1.0, F32)
        for o in range(NOFF):
            dy, dx = o // 3 - 1, o % 3 - 1
            picks = jnp.where((jy - iy == dy) & (jx - ix == dx), code[:, o:o + 1], picks)
        live = picks >= 0
        logits = jnp.where(live, logits, DEAD)
        e = jnp.where(live, jnp.exp(logits - jnp.max(logits, axis=-1, keepdims=True)), 0.0)
        prob = e / jnp.sum(e, axis=-1, keepdims=True)
        picks = jnp.where(live, picks, 0.0)
        count = jnp.sum(picks, axis=-1, keepdims=True)
        normal = float(TOPK * HEADS * nb) * math.sqrt(RW)
        dl = jnp.where(live, count * prob - picks, 0.0) / normal
        drq = jnp.dot(dl, rk, precision=HIGH, preferred_element_type=F32)
        drk = lax.dot_general(
            dl, rq, (((0,), (0,)), ((), ())), precision=HIGH, preferred_element_type=F32)
        grads = [
            lax.dot_general(
                a, b, (((0,), (0,)), ((), ())), precision=HIGH, preferred_element_type=F32)
            for a, b in ((drq, pq), (drk, pk))
        ]
        xbuf[img] = jnp.concatenate(grads, axis=0)
        for d in range(1, ni):
            x_copy(d).start()

    def g_copy(d, head):
        return pltpu.make_async_remote_copy(
            src_ref=gbuf.at[head], dst_ref=gbuf.at[head],
            send_sem=gs_sem.at[d], recv_sem=gr_sem.at[head],
            device_id={"px": lax.rem(px + d, npx)}, device_id_type=MESH,
        )

    def sum_images():
        @pl.when(own)
        def _():
            for d in range(1, ni):
                x_arrival(d).wait_recv()
            total = xbuf[0]
            for i in range(1, ni):
                total = total + xbuf[i]
            gbuf[my_head] = total.astype(BF16)
            for d in range(1, npx):
                g_copy(d, my_head).start()

    def h_copy(bit, start, count, slot):
        mate = py + bit - 2 * bit * lax.rem(lax.div(py, bit), 2)
        return pltpu.make_async_remote_copy(
            src_ref=gbuf.at[pl.ds(start, count)], dst_ref=gbuf.at[pl.ds(start, count)],
            send_sem=hs_sem.at[slot], recv_sem=hr_sem.at[slot],
            device_id={"py": mate}, device_id_type=MESH,
        )

    bits = []
    b = npy // 2
    while b:
        bits.append(b)
        b //= 2

    def held(step):
        found = [py]
        for s in range(step):
            bit = bits[s]
            found = found + [r + bit - 2 * bit * lax.rem(lax.div(r, bit), 2) for r in found]
        return found

    def slots(step):
        return [2 ** step - 1 + i for i in range(2 ** step)]

    def cube_send(step):
        for r, slot in zip(held(step), slots(step)):
            h_copy(bits[step], r * per_py, per_py, slot).start()

    def cube_wait(step):
        bit = bits[step]
        for r, slot in zip(held(step), slots(step)):
            other = r + bit - 2 * bit * lax.rem(lax.div(r, bit), 2)
            h_copy(bit, other * per_py, per_py, slot).wait_recv()

    def gather_px():
        for i in range(per_py):
            head = py * per_py + i
            @pl.when(jnp.logical_not(own & (my_head == head)))
            def _():
                g_copy(1, head).wait_recv()

    def finish_grads():
        def widen(h, carry):
            gq_s[h] = gbuf[h, 0:RW, :].astype(F32)
            gk_s[h] = gbuf[h, RW:2 * RW, :].astype(F32)
            return carry

        lax.fori_loop(0, HEADS, widen, 0)
        for store in grad_copies():
            store.start()

    def grad_copies():
        return [
            pltpu.make_async_copy(gq_s, gq_hbm, out_sem.at[NG]),
            pltpu.make_async_copy(gk_s, gk_hbm, out_sem.at[NG + 1]),
        ]

    def rim_heads(g):
        for j in range(HG):
            h = g * HG + j
            jl = pl.ds(j * DH, DH)
            q = q_s[h]
            qb = [q[i * BB:(i + 1) * BB] for i in range(4)]
            sx, sy, vx, vy = [], [], [], []
            for side in range(2):
                key = zr[side, g, 0, :, jl]
                sx.append(dot_t(jnp.concatenate([qb[side], qb[2 + side]], axis=0), key))
                vx.append(jnp.concatenate([zr[side, g, 1, :, jl], ones[:2 * BB]], axis=1))
                key = jnp.concatenate(
                    [yr[side, g, 0, :, :, jl].reshape(2 * BB, DH),
                     cr[side, 0, g, 0, :, jl], cr[side, 1, g, 0, :, jl]], axis=0)
                val = jnp.concatenate(
                    [yr[side, g, 1, :, :, jl].reshape(2 * BB, DH),
                     cr[side, 0, g, 1, :, jl], cr[side, 1, g, 1, :, jl]], axis=0)
                sy.append(dot_t(q[side * 2 * BB:(side + 1) * 2 * BB], key))
                vy.append(jnp.concatenate([val, ones], axis=1))
            wx, wy, ms = [], [], []
            for i in range(4):
                by, bx = divmod(i, 2)
                a = sx[bx][by * BB:(by + 1) * BB].reshape(BS, BS, 2 * BB)
                c = sy[by][bx * BB:(bx + 1) * BB].reshape(BS, BS, 4 * BB)
                a = jnp.minimum(a, cap_b[i, :, 0:2 * BB][None]).reshape(BB, 2 * BB)
                c = jnp.minimum(c, cap_b[i, :, 2 * BB:6 * BB][None]).reshape(BB, 4 * BB)
                widest = jnp.maximum(a, jnp.maximum(c[:, :2 * BB], c[:, 2 * BB:]))
                m = jnp.maximum(
                    top[h, i * BB:(i + 1) * BB, :], jnp.max(widest, axis=-1, keepdims=True))
                wx.append(jnp.exp2((a - m) * scale).astype(BF16))
                wy.append(jnp.exp2((c - jnp.concatenate([m, m], axis=1)) * scale).astype(BF16))
                ms.append(m)
            rx = [
                jnp.dot(jnp.concatenate([wx[s], wx[2 + s]], axis=0), vx[s],
                        preferred_element_type=F32)
                for s in range(2)
            ]
            ry = [
                jnp.dot(jnp.concatenate([wy[2 * s], wy[2 * s + 1]], axis=0), vy[s],
                        preferred_element_type=F32)
                for s in range(2)
            ]
            outs = []
            for i in range(4):
                by, bx = divmod(i, 2)
                rows = slice(i * BB, (i + 1) * BB)
                old = jnp.exp2((top[h, rows, :] - ms[i]) * scale)
                r = rx[bx][by * BB:(by + 1) * BB] + ry[by][bx * BB:(bx + 1) * BB]
                num = acc[h, rows, :] * old + r[:, :DH]
                tot = den[h, rows, :] * old + r[:, DH:]
                outs.append((num / tot).reshape(BS, BS, DH))
            for by in range(2):
                out_ref[by * BS:(by + 1) * BS, :, lanes(h * DH, DH)] = jnp.concatenate(
                    [outs[2 * by], outs[2 * by + 1]], axis=1).astype(BF16)
        out_copy(g).start()

    def out_copy(g):
        gl = lanes(g * GL, GL)
        return pltpu.make_async_copy(
            out_ref.at[:, :, gl], out_hbm.at[:, :, gl], out_sem.at[g])

    def advance(s, carry):
        @pl.when((s >= 2) & (s < NG))
        def _():
            forward(s)

        g = s - 1
        for side in range(2):
            @pl.when(has_y[side])
            def _():
                for which in range(2):
                    y_copy(which, side, g, side).wait_recv()
            for side_x in range(2):
                @pl.when(has_y[side] & has_x[side_x])
                def _():
                    c_copy(side, side_x, g, side).wait_recv()
        rim_heads(g)

        @pl.when(s == 1)
        def _():
            sum_images()
        @pl.when(s == 2)
        def _():
            gather_px()
            cube_send(0)
        for step in range(1, len(bits)):
            @pl.when(s == 2 + step)
            def _():
                cube_wait(step - 1)
                cube_send(step)
        @pl.when(s == 2 + len(bits))
        def _():
            cube_wait(len(bits) - 1)
            finish_grads()
        return carry

    lax.fori_loop(1, NG + 1, advance, 0)

    def drain(g, carry):
        for side in range(2):
            @pl.when(has_x[side])
            def _():
                z_copy(side, g).wait_send()
            @pl.when(has_y[side])
            def _():
                for which in range(2):
                    y_copy(which, side, g, 1 - side).wait_send()
            for side_x in range(2):
                @pl.when(has_y[side] & has_x[side_x])
                def _():
                    c_copy(side, side_x, g, 1 - side).wait_send()
        out_copy(g).wait()
        return carry

    lax.fori_loop(0, NG, drain, 0)
    for store in grad_copies():
        store.wait()
    for h in range(HEADS):
        oy, ox = owner_of(h)
        @pl.when(jnp.logical_not((py == oy) & (px == ox)))
        def _():
            m_copy(h, me).wait_send()
    @pl.when(own)
    def _():
        for d in range(1, ni):
            x_copy(d).wait_send()
        for d in range(1, npx):
            g_copy(d, my_head).wait_send()
    for step in range(len(bits)):
        for r, slot in zip(held(step), slots(step)):
            h_copy(bits[step], r * per_py, per_py, slot).wait_send()


def hand_over(*refs):
    count = len(refs) // 3
    come, go = refs[-2:]
    pieces, at = [], 0
    for src, dst, mid in zip(refs[:count], refs[count:2 * count], refs[2 * count:-2]):
        step = src.shape[0] // 4
        for i in range(4):
            rows = pl.ds(i * step, step)
            pieces.append((
                pltpu.make_async_copy(src.at[rows], mid.at[rows], come.at[at]),
                pltpu.make_async_copy(mid.at[rows], dst.at[rows], go.at[at]),
            ))
            at += 1
    for first, _ in pieces:
        first.start()
    for first, second in pieces:
        first.wait()
        second.start()
    for _, second in pieces:
        second.wait()


def per_device(sizes, queries, keys, values, pattern, targets, router_q, router_k):
    ni, npy, npx = sizes
    _, ty, tx, feat = queries.shape
    group = npy * npx
    dma = pltpu.SemaphoreType.DMA
    away = pl.BlockSpec(memory_space=pl.ANY)
    smem = pl.BlockSpec(memory_space=pltpu.SMEM)
    attended, grad_q, grad_k = pl.pallas_call(
        functools.partial(kernel, sizes),
        out_shape=(
            jax.ShapeDtypeStruct((ty, tx, feat), BF16),
            jax.ShapeDtypeStruct((HEADS, RW, DH), F32),
            jax.ShapeDtypeStruct((HEADS, RW, DH), F32),
        ),
        in_specs=[away, away, away, smem, smem, away, away],
        out_specs=(away, away, away),
        scratch_shapes=[
            pltpu.VMEM((ty, tx, feat), BF16),
            pltpu.VMEM((ty, tx, feat), BF16),
            pltpu.VMEM((ty, tx, feat), BF16),
            pltpu.VMEM((RW, DH), F32),
            pltpu.VMEM((RW, DH), F32),
            pltpu.VMEM((ty, tx, feat), BF16),
            pltpu.VMEM((HEADS, RW, DH), F32),
            pltpu.VMEM((HEADS, RW, DH), F32),
            pltpu.VMEM((HEADS, 4 * BB, DH), BF16),
            pltpu.VMEM((2, NG, 2, 2 * BB, GL), BF16),
            pltpu.VMEM((2, NG, 2, 2 * BB, GL), BF16),
            pltpu.VMEM((2, NG, 2, BS, 2 * BS, GL), BF16),
            pltpu.VMEM((2, 2, NG, 2, BB, GL), BF16),
            pltpu.VMEM((HEADS, 4 * BB, DH), F32),
            pltpu.VMEM((HEADS, 4 * BB, DH), F32),
            pltpu.VMEM((HEADS, 4 * BB, DH), F32),
            pltpu.VMEM((4, BS, 4 * BB), F32),
            pltpu.VMEM((4, BS, 6 * BB), F32),
            pltpu.VMEM((HEADS, 16, DH), F32),
            pltpu.VMEM((group, 16, DH), F32),
            pltpu.VMEM((ni, 2 * RW, DH), F32),
            pltpu.VMEM((HEADS, 2 * RW, DH), BF16),
            dma((2, NG)), dma((2, NG)),
            dma((2, 2, NG)), dma((2, 2, NG)),
            dma((2, 2, NG)), dma((2, 2, NG)),
            dma((HEADS,)), dma((group,)),
            dma((ni,)), dma((ni,)),
            dma((npx,)), dma((HEADS,)),
            dma((npy,)), dma((npy,)), dma((5,)), dma((NG + 2,)),
        ],
        compiler_params=pltpu.CompilerParams(
            collective_id=0, has_side_effects=True, vmem_limit_bytes=56 * 2 ** 20
        ),
    )(
        queries[0], keys[0], values[0], pattern, jnp.transpose(targets, (0, 1, 4, 2, 3)),
        jnp.swapaxes(router_q, 1, 2), jnp.swapaxes(router_k, 1, 2),
    )
    made = (attended, grad_q, grad_k)
    attended, grad_q, grad_k = pl.pallas_call(
        hand_over,
        out_shape=tuple(jax.ShapeDtypeStruct(a.shape, a.dtype) for a in made),
        in_specs=[away] * 3,
        out_specs=(away,) * 3,
        scratch_shapes=[pltpu.VMEM(a.shape, a.dtype) for a in made] + [dma((12,)), dma((12,))],
        compiler_params=pltpu.CompilerParams(vmem_limit_bytes=56 * 2 ** 20),
    )(*made)
    return attended[None], jnp.swapaxes(grad_q, 1, 2), jnp.swapaxes(grad_k, 1, 2)


def solution(mesh):
    sizes = tuple(mesh.shape[a] for a in ("img", "py", "px"))
    return jax.shard_map(
        functools.partial(per_device, sizes),
        mesh=mesh,
        in_specs=(
            P("img", "py", "px", None),
            P("img", "py", "px", None),
            P("img", "py", "px", None),
            P("img", "py", "px", None),
            P("img", "py", "px", None, None),
            P(),
            P(),
        ),
        out_specs=(P("img", "py", "px", None), P(), P()),
        check_vma=False,
    )
```
